32 devices in a mesh: ckpt: 2 (over x), fsdp: 16 (over z, y, core).
Axes of the slice: x: 2, y: 2, z: 4, core: 2. Of those that a mesh axis runs over, the one named last changes fastest.
Arguments:
- tokens: bfloat16 [2, 128, 4096], P('ckpt', 'fsdp'), may hold values from -6 to 6
- gate_weight: bfloat16 [2, 14336, 4096], P('ckpt', 'fsdp'), may hold values from -6 to 6
- up_weight: bfloat16 [2, 14336, 4096], P('ckpt', 'fsdp'), may hold values from -6 to 6
- down_weight: bfloat16 [2, 14336, 4096], P('ckpt', 'fsdp'), may hold values from -0.046875 to 0.046875
- row_code: int32 [2, 2, 4096], P('ckpt'), may hold values from 0 to 2097151
- col_code: int32 [2, 2, 14336], P('ckpt', None, 'fsdp'), may hold values from 0 to 2097151
Outputs:
- merged_gate: bfloat16 [14336, 4096], P('fsdp', 'ckpt')
- merged_up: bfloat16 [14336, 4096], P('fsdp', 'ckpt')
The draws below stay inside these ranges and needn't reach their ends.
All inputs are finite; a program needn't handle non-finite values.
Results may differ from the reference program's by a relative error of at most 0.028.
Values may be sent and summed in bfloat16 or wider, within the bound.
No kernel may reach another device: no remote copies, remote signals or barrier semaphores. Data moves between devices by JAX's collectives and lax.ppermute only.
A program may use at most 128 MiB of HBM per device.

```python
import jax
import jax.numpy as jnp
from jax import lax

D = 4096
FF = 14336
TOKENS = 128
CKPT = 2
N_CKPT = 2


def set_ends(entries, stream_key, low, top_value):
    dims = entries.shape
    spot = [jax.random.randint(jax.random.fold_in(stream_key, axis), (), 0, dims[axis]) for axis in range(len(dims))]
    entries = entries.at[tuple(spot)].set(low)
    longest = dims.index(max(dims))
    spot[longest] = (spot[longest] + 1) % dims[longest]
    return entries.at[tuple(spot)].set(top_value)


def levels(key, extent, split, smallest, largest):
    def one(axis_at, parts):
        draws = jax.random.uniform(jax.random.fold_in(jax.random.fold_in(key, 6), axis_at), (parts,), jnp.float32, smallest / len(split), largest / len(split))
        return jnp.repeat(jnp.exp(draws), extent[axis_at] // parts).reshape((-1,) + (1,) * (len(extent) - axis_at - 1))

    level = one(*split[0])
    for cut in split[1:]:
        level = level * one(*cut)
    return level


def centred(key, shape, spread, reach, pieces=(), kind=jnp.bfloat16):
    factor_of = levels(key, shape, pieces, -0.22, 0.18) if pieces else 1.0
    array = jax.random.normal(key, shape, jnp.float32) * spread * factor_of
    return jnp.minimum(jnp.maximum(array, -reach), reach).astype(kind)


def setup_inputs(seed: int = 0) -> dict:
    key_of = jax.random.split(jax.random.key(seed), 7)
    tokens = centred(key_of[0], (CKPT, TOKENS, D), 1.0, 6.0, ((0, 2), (1, 16)))
    gate_weight = centred(key_of[1], (CKPT, FF, D), 1.0, 6.0, ((0, 2), (1, 16)))
    up_weight = centred(key_of[2], (CKPT, FF, D), 1.0, 6.0, ((0, 2), (1, 16)))
    down_weight = centred(key_of[3], (CKPT, FF, D), FF ** -0.5, 0.046875, ((0, 2), (1, 16)))
    row_code = set_ends(jax.random.randint(key_of[4], (CKPT, 2, D), 0, 2097152), jax.random.fold_in(key_of[4], 1), 0, 2097151).astype(jnp.int32)
    col_code = set_ends(jax.random.randint(key_of[5], (CKPT, 2, FF), 0, 2097152), jax.random.fold_in(key_of[5], 1), 0, 2097151).astype(jnp.int32)
    return dict(tokens=tokens, gate_weight=gate_weight, up_weight=up_weight, down_weight=down_weight, row_code=row_code, col_code=col_code)


def odd_bits(value):
    for shift in (16, 8, 4, 2, 1):
        value = jnp.bitwise_xor(value, jnp.right_shift(value, shift))
    return jnp.bitwise_and(value, 1)


def probe(col, row):
    bits = odd_bits(jnp.bitwise_and(col[:, None], row[None, :]))
    return (1 - 2 * bits).astype(jnp.bfloat16)


def cross(left, right):
    return lax.dot_general(left, right, (((1,), (1,)), ((), ())), preferred_element_type=jnp.float32)


def inner(left, right):
    return lax.dot_general(left, right, (((0,), (0,)), ((), ())), preferred_element_type=jnp.float32)


def merge_weight(hessian, signs):
    magnitude = jnp.abs(signs.astype(jnp.float32) * hessian)
    return magnitude / (jnp.mean(magnitude, axis=1, keepdims=True) + 1e-6)


def rounded(value):
    return lax.optimization_barrier(value.astype(jnp.bfloat16)).astype(jnp.float32)


def reference(tokens, gate_weight, up_weight, down_weight, row_code, col_code):
    shape = (FF, D)
    num_gate = jnp.zeros(shape, jnp.float32)
    den_gate = jnp.zeros(shape, jnp.float32)
    num_up = jnp.zeros(shape, jnp.float32)
    den_up = jnp.zeros(shape, jnp.float32)
    factor = D ** -0.5
    for member in range(N_CKPT):
        whole = tokens[member]
        gate = gate_weight[member]
        upper = up_weight[member]
        down = down_weight[member]
        z_gate = probe(col_code[member, 0], row_code[member, 0])
        z_up = probe(col_code[member, 1], row_code[member, 1])
        a_pre = cross(gate, whole) * factor
        b_pre = cross(upper, whole) * factor
        da_pre = cross(z_gate, whole) * factor
        db_pre = cross(z_up, whole) * factor
        sigma = jax.nn.sigmoid(a_pre)
        act = a_pre * sigma
        slope = sigma * (1.0 + a_pre * (1.0 - sigma))
        curve = sigma * (1.0 - sigma) * (2.0 + a_pre * (1.0 - 2.0 * sigma))
        hidden = (act * b_pre).astype(jnp.bfloat16)
        d_hidden = (slope * da_pre * b_pre + act * db_pre).astype(jnp.bfloat16)
        out_y = inner(hidden, down)
        out_dy = inner(d_hidden, down)
        grad_y = out_y.astype(jnp.bfloat16)
        grad_dy = out_dy.astype(jnp.bfloat16)
        grad_h = cross(down, grad_y)
        grad_dh = cross(down, grad_dy)
        dga = (grad_dh * b_pre * slope + grad_h * db_pre * slope + grad_h * b_pre * curve * da_pre).astype(jnp.bfloat16)
        dgb = (grad_dh * act + grad_h * slope * da_pre).astype(jnp.bfloat16)
        hz_gate = jnp.dot(dga, whole, preferred_element_type=jnp.float32)
        hz_up = jnp.dot(dgb, whole, preferred_element_type=jnp.float32)
        w_gate = merge_weight(hz_gate, z_gate)
        w_up = merge_weight(hz_up, z_up)
        num_gate = num_gate + rounded(w_gate * gate.astype(jnp.float32))
        den_gate = den_gate + rounded(w_gate)
        num_up = num_up + rounded(w_up * upper.astype(jnp.float32))
        den_up = den_up + rounded(w_up)
    merged_gate = (num_gate / jnp.maximum(den_gate, 1.0)).astype(jnp.bfloat16)
    merged_up = (num_up / jnp.maximum(den_up, 1.0)).astype(jnp.bfloat16)
    return merged_gate, merged_up
```

```python
import functools

import jax
import jax.numpy as jnp
from jax import lax
from jax.experimental import pallas as pl
from jax.experimental.pallas import tpu as pltpu
from jax.sharding import PartitionSpec as P

F32 = jnp.float32
BF16 = jnp.bfloat16
NT = (((1,), (1,)), ((), ()))
NN = (((1,), (0,)), ((), ()))
TN = (((0,), (0,)), ((), ()))


def dot(left, right, dims):
    return lax.dot_general(left, right, dims, preferred_element_type=F32)


def params():
    return pltpu.CompilerParams(
        dimension_semantics=("arbitrary",), vmem_limit_bytes=48 * 1024 * 1024
    )


def rows_of(units):
    return 128 if units % 128 == 0 else units


def tile_of(width):
    return 512 if width % 512 == 0 else width


def hops(n):
    high = list(range(1, n.bit_length() - 1))
    return list(zip(high, high[1:] + high[:1]))


def swap(value, axis, n, even, odd):
    pairs = [(i, i ^ (1 << (odd if i & 1 else even))) for i in range(n)]
    return lax.ppermute(value, axis, pairs)


def side(axis, even, odd):
    me = lax.axis_index(axis)
    return jnp.where(me & 1 == 1, (me >> odd) & 1, (me >> even) & 1)


def add(left, right):
    return (left.astype(F32) + right.astype(F32)).astype(BF16)


def scatter_sum(value, axis, n):
    for even, odd in hops(n):
        half = value.shape[0] // 2
        mine = side(axis, even, odd)
        keep = lax.dynamic_slice_in_dim(value, mine * half, half, 0)
        send = lax.dynamic_slice_in_dim(value, (1 - mine) * half, half, 0)
        value = add(keep, swap(send, axis, n, even, odd))
    return value


def gather(value, axis, n):
    for even, odd in reversed(hops(n)):
        other = swap(value, axis, n, even, odd)
        first = side(axis, even, odd) == 0
        value = jnp.where(
            first, jnp.concatenate([value, other]), jnp.concatenate([other, value])
        )
    return value


def gather_order(n):
    order = []
    for core in (0, 1):
        bits = [pair[core] for pair in reversed(hops(n))]
        for place in range(n // 2):
            order.append(core + sum(((place >> j) & 1) << b for j, b in enumerate(bits)))
    return order


def forward_kernel(factor, steps, core, x, gate, upper, down, row, col, p, q, act, sd,
                   send, keep, hid, whole, sem):
    step = pl.program_id(0)
    tokens, width = x.shape
    units = gate.shape[0]
    copy = pltpu.make_async_copy(down, whole, sem)

    @pl.when(step == 0)
    def _():
        copy.start()

    a = dot(x[...], gate[...], NT) * factor
    b = dot(x[...], upper[...], NT) * factor
    tile = tile_of(width)
    da = jnp.zeros((tokens, units), F32)
    db = jnp.zeros((tokens, units), F32)
    for at in range(0, width, tile):
        part = x[:, at:at + tile]
        signs = []
        for k in (0, 1):
            code = jnp.bitwise_and(col[:, k:k + 1], row[k:k + 1, at:at + tile])
            odd = jnp.bitwise_and(lax.population_count(code), 1)
            signs.append((1 - 2 * odd).astype(F32).astype(BF16))
        da = da + dot(part, signs[0], NT)
        db = db + dot(part, signs[1], NT)
    da = da * factor
    db = db * factor
    sigma = jax.nn.sigmoid(a)
    s = a * sigma
    slope = sigma * (1.0 + a * (1.0 - sigma))
    curve = sigma * (1.0 - sigma) * (2.0 + a * (1.0 - 2.0 * sigma))
    p[...] = b * slope
    q[...] = db * slope + b * curve * da
    act[...] = s
    sd[...] = slope * da
    hidden = s * b
    d_hidden = slope * da * b + s * db
    even = core[0] == 0
    if steps == 1:
        place = slice(None)
    else:
        place = pl.ds(pl.multiple_of(step * units, units), units)
    hid[:tokens, place] = jnp.where(even, d_hidden, hidden).astype(BF16)
    hid[tokens:, place] = jnp.where(even, hidden, d_hidden).astype(BF16)

    @pl.when(step == steps - 1)
    def _():
        copy.wait()
        for at in range(0, width, tile):
            both = dot(hid[...], whole[:, at:at + tile], NN)
            send[:, at:at + tile] = both[:tokens].astype(BF16)
            keep[:, at:at + tile] = both[tokens:].astype(BF16)


def forward(core, x, gate, upper, down, row, col):
    tokens, width = x.shape
    units = gate.shape[0]
    block = rows_of(units)
    steps = units // block
    by_unit = pl.BlockSpec((block, width), lambda i, c: (i, 0))
    by_lane = pl.BlockSpec((tokens, block), lambda i, c: (0, i))
    fixed = pl.BlockSpec((tokens, width), lambda i, c: (0, 0))
    wide = jax.ShapeDtypeStruct((tokens, units), F32)
    out = jax.ShapeDtypeStruct((tokens, width), BF16)
    return pl.pallas_call(
        functools.partial(forward_kernel, width ** (-0.5), steps),
        out_shape=(wide,) * 4 + (out,) * 2,
        grid_spec=pltpu.PrefetchScalarGridSpec(
            num_scalar_prefetch=1,
            grid=(steps,),
            in_specs=[
                fixed,
                by_unit,
                by_unit,
                pl.BlockSpec(memory_space=pl.ANY),
                pl.BlockSpec((2, width), lambda i, c: (0, 0)),
                pl.BlockSpec((block, 2), lambda i, c: (i, 0)),
            ],
            out_specs=[by_lane] * 4 + [fixed] * 2,
            scratch_shapes=[
                pltpu.VMEM((2 * tokens, units), BF16),
                pltpu.VMEM((units, width), BF16),
                pltpu.SemaphoreType.DMA,
            ],
        ),
        compiler_params=params(),
        cost_estimate=pl.CostEstimate(
            flops=12 * tokens * width * units,
            bytes_accessed=6 * units * width,
            transcendentals=tokens * units,
        ),
        name="forward",
    )(core, x, gate, upper, down, row, col)


def backward_kernel(core, mine, other, down, x, p, q, act, sd, grads, scale):
    tokens, width = x.shape
    units = down.shape[0]
    g_mine = dot(mine[...], down[...], NT)
    g_other = dot(other[...], down[...], NT)
    even = core[0] == 0
    gh = jnp.where(even, g_mine, g_other)
    gdh = jnp.where(even, g_other, g_mine)
    both = (
        (gdh * p[...] + gh * q[...]).astype(BF16),
        (gdh * act[...] + gh * sd[...]).astype(BF16),
    )
    tile = tile_of(width)
    lanes = 128 if tile % 128 == 0 else tile
    rows = []
    for k, grad in enumerate(both):
        grads[k * tokens:(k + 1) * tokens, :] = grad
        total = jnp.zeros((units, lanes), F32)
        for at in range(0, width, tile):
            e = jnp.abs(dot(grad, x[:, at:at + tile], TN))
            for low in range(0, tile, lanes):
                total = total + e[:, low:low + lanes]
        mean = jnp.sum(total.T, axis=0, keepdims=True) * (1.0 / width)
        rows.append(1.0 / (mean + 1e-06))
    scale[...] = jnp.concatenate(rows + [jnp.zeros((6, units), F32)], axis=0)


def backward(core, mine, other, down, x, kept):
    tokens, width = x.shape
    units = down.shape[0]
    block = rows_of(units)
    by_lane = pl.BlockSpec((tokens, block), lambda i, c: (0, i))
    fixed = pl.BlockSpec((tokens, width), lambda i, c: (0, 0))
    return pl.pallas_call(
        backward_kernel,
        out_shape=(
            jax.ShapeDtypeStruct((2 * tokens, units), BF16),
            jax.ShapeDtypeStruct((8, units), F32),
        ),
        grid_spec=pltpu.PrefetchScalarGridSpec(
            num_scalar_prefetch=1,
            grid=(units // block,),
            in_specs=[
                fixed,
                fixed,
                pl.BlockSpec((block, width), lambda i, c: (i, 0)),
                fixed,
            ] + [by_lane] * 4,
            out_specs=[
                pl.BlockSpec((2 * tokens, block), lambda i, c: (0, i)),
                pl.BlockSpec((8, block), lambda i, c: (0, i)),
            ],
        ),
        compiler_params=params(),
        cost_estimate=pl.CostEstimate(
            flops=8 * tokens * width * units,
            bytes_accessed=2 * units * width,
            transcendentals=0,
        ),
        name="backward",
    )(core, mine, other, down, x, *kept)


def merge_kernel(which, members, *refs):
    refs = refs[1:]
    weights, refs = refs[:members], refs[members:]
    grads, refs = refs[:members], refs[members:]
    scales, refs = refs[:members], refs[members:]
    tokens = refs[:members]
    out = refs[-1]
    width = out.shape[1]
    tile = tile_of(width)
    columns = [scale[...].T[:, which:which + 1] for scale in scales]
    for at in range(0, width, tile):
        numer = denom = None
        for j in range(members):
            hz = dot(grads[j][...], tokens[j][:, at:at + tile], TN)
            w = jnp.abs(hz) * columns[j]
            term = (w * weights[j][:, at:at + tile].astype(F32)).astype(BF16).astype(F32)
            w = w.astype(BF16).astype(F32)
            numer = term if numer is None else numer + term
            denom = w if denom is None else denom + w
        out[:, at:at + tile] = (numer / jnp.maximum(denom, 1.0)).astype(BF16)


def merge(spot, which, start, weight, received, grads, scales, x, others, so_far):
    members = 1 + len(received)
    units = weight.shape[0]
    tokens, width = others[0].shape
    block = rows_of(units)
    rows = received[0].shape[0]
    first = start // block
    in_specs = [pl.BlockSpec((block, width), lambda i, c: (first + i, c[0]))]
    in_specs += [pl.BlockSpec((block, width), lambda i, c: (i, 0))] * (members - 1)
    in_specs += [pl.BlockSpec((tokens, block), lambda i, c: (which, first + i))] * members
    in_specs += [pl.BlockSpec((8, block), lambda i, c: (0, first + i))] * members
    in_specs += [pl.BlockSpec((tokens, width), lambda i, c: (0, c[0]))]
    in_specs += [pl.BlockSpec((tokens, width), lambda i, c: (0, 0))] * (members - 1)
    args = [spot, weight, *received, *grads, *scales, x, *others]
    aliases = {}
    if so_far is not None:
        aliases = {len(args): 0}
        in_specs.append(pl.BlockSpec(memory_space=pl.ANY))
        args.append(so_far)
    return pl.pallas_call(
        functools.partial(merge_kernel, which, members),
        out_shape=jax.ShapeDtypeStruct((units, width), BF16),
        grid_spec=pltpu.PrefetchScalarGridSpec(
            num_scalar_prefetch=1,
            grid=(rows // block,),
            in_specs=in_specs,
            out_specs=pl.BlockSpec((block, width), lambda i, c: (first + i, 0)),
        ),
        input_output_aliases=aliases,
        compiler_params=params(),
        cost_estimate=pl.CostEstimate(
            flops=2 * members * tokens * width * rows,
            bytes_accessed=2 * (members + 1) * rows * width,
            transcendentals=0,
        ),
        name="merge",
    )(*args)


def pieces(units):
    block = rows_of(units)
    count = units // block
    if count < 4:
        return [(0, 0, units), (1, 0, units)], []
    last = block
    third = block * max(1, count // 3)
    head = units - last - third
    return (
        [(0, 0, units), (1, 0, head)],
        [(1, head, third), (1, head + third, last)],
    )


def on_device(n_ckpt, n_fsdp, tokens, gate_weight, up_weight, down_weight, row_code, col_code):
    weights = (gate_weight[0], up_weight[0])
    down = down_weight[0]
    own = tokens[0]
    units, width = down.shape
    part = width // n_ckpt
    spot = lax.axis_index("ckpt")
    core = (lax.axis_index("fsdp") & 1).astype(jnp.int32).reshape(1)
    at = spot.astype(jnp.int32).reshape(1)

    def across(value, shift):
        return lax.ppermute(
            value, "ckpt", [(i, (i + shift) % n_ckpt) for i in range(n_ckpt)]
        )

    def cut(which, start, rows, shift):
        left = lax.rem(spot + shift, n_ckpt) * part
        return lax.dynamic_slice(weights[which], (start, left), (rows, part))

    shifts = range(1, n_ckpt)
    early, late = pieces(units)
    arrived = {}
    for piece in early:
        arrived[piece] = [across(cut(*piece, s), s) for s in shifts]

    x = gather(own, "fsdp", n_fsdp)
    other = lax.ppermute(x, "fsdp", [(i, i ^ 1) for i in range(n_fsdp)])
    even = core[0] == 0
    x = jnp.where(even, jnp.concatenate([x, other]), jnp.concatenate([other, x]))

    others = []
    order = gather_order(n_fsdp)
    for s in shifts:
        left = lax.rem(spot + s, n_ckpt) * part
        mine = lax.dynamic_slice(own, (0, left), (own.shape[0], part))
        natural = lax.all_gather(across(mine, s), "fsdp", axis=0, tiled=False)
        others.append(jnp.concatenate([natural[i] for i in order]))

    *kept, send, keep = forward(
        core, x, weights[0], weights[1], down, row_code[0], col_code[0].T
    )
    got = lax.ppermute(send, "fsdp", [(i, i ^ 1) for i in range(n_fsdp)])
    total = gather(scatter_sum(add(keep, got), "fsdp", n_fsdp), "fsdp", n_fsdp)
    other = lax.ppermute(total, "fsdp", [(i, i ^ 1) for i in range(n_fsdp)])
    grads, scale = backward(core, total, other, down, x, kept)

    all_grads = [grads] + [across(grads, s) for s in shifts]
    all_scales = [scale] + [across(scale, s) for s in shifts]
    for piece in late:
        blocks, _ = lax.optimization_barrier(([cut(*piece, s) for s in shifts], grads))
        arrived[piece] = [across(block, s) for block, s in zip(blocks, shifts)]

    out = [None, None]
    for which, start, rows in early + late:
        out[which] = merge(
            at, which, start, weights[which], arrived[which, start, rows], all_grads,
            all_scales, x, others, out[which],
        )
    return tuple(out)


def solution(mesh):
    in_specs = (
        P("ckpt", "fsdp", None),
        P("ckpt", "fsdp", None),
        P("ckpt", "fsdp", None),
        P("ckpt", "fsdp", None),
        P("ckpt", None, None),
        P("ckpt", None, "fsdp"),
    )
    out_specs = (P("fsdp", "ckpt"), P("fsdp", "ckpt"))
    return jax.shard_map(
        functools.partial(on_device, mesh.shape["ckpt"], mesh.shape["fsdp"]),
        mesh=mesh, in_specs=in_specs, out_specs=out_specs, check_vma=False,
    )
```

```python
import functools
import math

import jax
import jax.numpy as jnp
from jax import lax
from jax.experimental import pallas as pl
from jax.experimental.pallas import tpu as pltpu
from jax.sharding import PartitionSpec as P

F32 = jnp.float32
BF16 = jnp.bfloat16
LANES = 128
NT = (((1,), (1,)), ((), ()))
NN = (((1,), (0,)), ((), ()))
TN = (((0,), (0,)), ((), ()))


def dot(left, right, dims):
    return lax.dot_general(left, right, dims, preferred_element_type=F32)


def params():
    return pltpu.CompilerParams(
        dimension_semantics=("arbitrary",), vmem_limit_bytes=48 * 1024 * 1024
    )


def rows_of(units):
    return 128 if units % 128 == 0 else units


def tile_of(width):
    return 512 if width % 512 == 0 else width


def hops(n):
    high = list(range(1, n.bit_length() - 1))
    return list(zip(high, high[1:] + high[:1]))


def swap(value, axis, n, even, odd):
    pairs = [(i, i ^ (1 << (odd if i & 1 else even))) for i in range(n)]
    return lax.ppermute(value, axis, pairs)


def side(axis, even, odd):
    me = lax.axis_index(axis)
    return jnp.where(me & 1 == 1, (me >> odd) & 1, (me >> even) & 1)


def add(left, right):
    return (left.astype(F32) + right.astype(F32)).astype(BF16)


def scatter_sum(value, axis, n):
    for even, odd in hops(n):
        half = value.shape[0] // 2
        mine = side(axis, even, odd)
        keep = lax.dynamic_slice_in_dim(value, mine * half, half, 0)
        send = lax.dynamic_slice_in_dim(value, (1 - mine) * half, half, 0)
        value = add(keep, swap(send, axis, n, even, odd))
    return value


def gather(value, axis, n, plan, after=lambda step, value: value):
    for step, (even, odd) in enumerate(reversed(plan)):
        other = swap(value, axis, n, even, odd)
        first = side(axis, even, odd) == 0
        value = jnp.where(
            first, jnp.concatenate([value, other]), jnp.concatenate([other, value])
        )
        value = after(step, value)
    return value


def gather_order(n, plan):
    order = []
    for core in (0, 1):
        bits = [pair[core] for pair in reversed(plan)]
        for place in range(n // 2):
            order.append(core + sum(((place >> j) & 1) << b for j, b in enumerate(bits)))
    return order


def forward_kernel(factor, steps, core, x, gate, upper, down, row, col, p, q, act, sd,
                   send, keep, hid, whole, sem):
    step = pl.program_id(0)
    tokens, width = x.shape
    units = gate.shape[0]
    copy = pltpu.make_async_copy(down, whole, sem)

    @pl.when(step == 0)
    def _():
        copy.start()

    a = dot(x[...], gate[...], NT) * factor
    b = dot(x[...], upper[...], NT) * factor
    tile = tile_of(width)
    da = jnp.zeros((tokens, units), F32)
    db = jnp.zeros((tokens, units), F32)
    for at in range(0, width, tile):
        part = x[:, at:at + tile]
        signs = []
        for k in (0, 1):
            code = jnp.bitwise_and(col[:, k:k + 1], row[k:k + 1, at:at + tile])
            odd = jnp.bitwise_and(lax.population_count(code), 1)
            signs.append((1 - 2 * odd).astype(F32).astype(BF16))
        da = da + dot(part, signs[0], NT)
        db = db + dot(part, signs[1], NT)
    da = da * factor
    db = db * factor
    sigma = jax.nn.sigmoid(a)
    s = a * sigma
    slope = sigma * (1.0 + a * (1.0 - sigma))
    curve = sigma * (1.0 - sigma) * (2.0 + a * (1.0 - 2.0 * sigma))
    p[...] = b * slope
    q[...] = db * slope + b * curve * da
    act[...] = s
    sd[...] = slope * da
    hidden = s * b
    d_hidden = slope * da * b + s * db
    even = core[0] == 0
    if steps == 1:
        place = slice(None)
    else:
        place = pl.ds(pl.multiple_of(step * units, units), units)
    hid[:tokens, place] = jnp.where(even, d_hidden, hidden).astype(BF16)
    hid[tokens:, place] = jnp.where(even, hidden, d_hidden).astype(BF16)

    @pl.when(step == steps - 1)
    def _():
        copy.wait()
        for at in range(0, width, tile):
            both = dot(hid[...], whole[:, at:at + tile], NN)
            send[:, at:at + tile] = both[:tokens].astype(BF16)
            keep[:, at:at + tile] = both[tokens:].astype(BF16)


def forward(core, x, gate, upper, down, row, col):
    tokens, width = x.shape
    units = gate.shape[0]
    block = rows_of(units)
    steps = units // block
    by_unit = pl.BlockSpec((block, width), lambda i, c: (i, 0))
    by_lane = pl.BlockSpec((tokens, block), lambda i, c: (0, i))
    fixed = pl.BlockSpec((tokens, width), lambda i, c: (0, 0))
    wide = jax.ShapeDtypeStruct((tokens, units), F32)
    out = jax.ShapeDtypeStruct((tokens, width), BF16)
    return pl.pallas_call(
        functools.partial(forward_kernel, width ** (-0.5), steps),
        out_shape=(wide,) * 4 + (out,) * 2,
        grid_spec=pltpu.PrefetchScalarGridSpec(
            num_scalar_prefetch=1,
            grid=(steps,),
            in_specs=[
                fixed,
                by_unit,
                by_unit,
                pl.BlockSpec(memory_space=pl.ANY),
                pl.BlockSpec((2, width), lambda i, c: (0, 0)),
                pl.BlockSpec((block, 2), lambda i, c: (i, 0)),
            ],
            out_specs=[by_lane] * 4 + [fixed] * 2,
            scratch_shapes=[
                pltpu.VMEM((2 * tokens, units), BF16),
                pltpu.VMEM((units, width), BF16),
                pltpu.SemaphoreType.DMA,
            ],
        ),
        compiler_params=params(),
        cost_estimate=pl.CostEstimate(
            flops=12 * tokens * width * units,
            bytes_accessed=6 * units * width,
            transcendentals=tokens * units,
        ),
        name="forward",
    )(core, x, gate, upper, down, row, col)


def backward_kernel(core, mine, other, down, p, q, act, sd, grads):
    tokens = mine.shape[0]
    g_mine = dot(mine[...], down[...], NT)
    g_other = dot(other[...], down[...], NT)
    even = core[0] == 0
    gh = jnp.where(even, g_mine, g_other)
    gdh = jnp.where(even, g_other, g_mine)
    grads[:, :tokens] = (gdh * p[...] + gh * q[...]).T.astype(BF16)
    grads[:, tokens:] = (gdh * act[...] + gh * sd[...]).T.astype(BF16)


def backward(core, mine, other, down, kept):
    tokens, width = mine.shape
    units = down.shape[0]
    block = rows_of(units)
    by_lane = pl.BlockSpec((tokens, block), lambda i, c: (0, i))
    fixed = pl.BlockSpec((tokens, width), lambda i, c: (0, 0))
    return pl.pallas_call(
        backward_kernel,
        out_shape=jax.ShapeDtypeStruct((units, 2 * tokens), BF16),
        grid_spec=pltpu.PrefetchScalarGridSpec(
            num_scalar_prefetch=1,
            grid=(units // block,),
            in_specs=[
                fixed,
                fixed,
                pl.BlockSpec((block, width), lambda i, c: (i, 0)),
            ] + [by_lane] * 4,
            out_specs=pl.BlockSpec((block, 2 * tokens), lambda i, c: (i, 0)),
        ),
        compiler_params=params(),
        cost_estimate=pl.CostEstimate(
            flops=4 * tokens * width * units,
            bytes_accessed=2 * units * width,
            transcendentals=0,
        ),
        name="backward",
    )(core, mine, other, down, *kept)


def means_kernel(grads, x, scale):
    tokens, width = x.shape
    units = grads.shape[0]
    tile = tile_of(width)
    for k in (0, 1):
        grad = grads[:, k * tokens:(k + 1) * tokens]
        total = jnp.zeros((units, LANES), F32)
        for at in range(0, width, tile):
            e = jnp.abs(dot(grad, x[:, at:at + tile], NN))
            for low in range(0, tile, LANES):
                total = total + e[:, low:low + LANES]
        mean = jnp.sum(total, axis=1, keepdims=True) * (1.0 / width)
        scale[:, k * LANES:(k + 1) * LANES] = jnp.broadcast_to(
            1.0 / (mean + 1e-06), (units, LANES)
        )


def means(grads, x):
    tokens, width = x.shape
    units = grads.shape[0]
    block = rows_of(units)
    return pl.pallas_call(
        means_kernel,
        out_shape=jax.ShapeDtypeStruct((units, 2 * LANES), F32),
        grid=(units // block,),
        in_specs=[
            pl.BlockSpec((block, 2 * tokens), lambda i: (i, 0)),
            pl.BlockSpec((tokens, width), lambda i: (0, 0)),
        ],
        out_specs=pl.BlockSpec((block, 2 * LANES), lambda i: (i, 0)),
        compiler_params=params(),
        cost_estimate=pl.CostEstimate(
            flops=4 * tokens * width * units,
            bytes_accessed=2 * tokens * width,
            transcendentals=0,
        ),
        name="means",
    )(grads, x)


def merge_kernel(members, *refs):
    refs = refs[1:]
    weights, refs = refs[:members], refs[members:]
    grads, refs = refs[:members], refs[members:]
    scales, refs = refs[:members], refs[members:]
    tokens = refs[:members]
    out = refs[-1]
    width = out.shape[1]
    tile = tile_of(width)
    columns = [scale[:, :1] for scale in scales]
    for at in range(0, width, tile):
        numer = denom = None
        for j in range(members):
            hz = dot(grads[j][...], tokens[j][:, at:at + tile], NN)
            w = jnp.abs(hz) * columns[j]
            term = (w * weights[j][:, at:at + tile].astype(F32)).astype(BF16).astype(F32)
            w = w.astype(BF16).astype(F32)
            numer = term if numer is None else numer + term
            denom = w if denom is None else denom + w
        out[:, at:at + tile] = (numer / jnp.maximum(denom, 1.0)).astype(BF16)


def merge(spot, piece, weight, received, grads, scales, xs, so_far):
    which, start, rows = piece
    members = len(xs)
    units = weight.shape[0]
    tokens = xs[0].shape[0]
    width = received[0].shape[1]
    block = math.gcd(rows, start, 128 if rows > 256 else 32)
    first = start // block
    in_specs = [pl.BlockSpec((block, width), lambda i, c: (first + i, c[0]))]
    in_specs += [pl.BlockSpec((block, width), lambda i, c: (i, 0))] * (members - 1)
    in_specs += [pl.BlockSpec((block, tokens), lambda i, c: (first + i, which))] * members
    in_specs += [pl.BlockSpec((block, LANES), lambda i, c: (first + i, which))] * members
    in_specs += [pl.BlockSpec((tokens, width), lambda i, c: (0, c[0]))] * members
    args = [spot, weight, *received, *grads, *scales, *xs]
    aliases = {}
    if so_far is not None:
        aliases = {len(args): 0}
        in_specs.append(pl.BlockSpec(memory_space=pl.ANY))
        args.append(so_far)
    return pl.pallas_call(
        functools.partial(merge_kernel, members),
        out_shape=jax.ShapeDtypeStruct((units, width), BF16),
        grid_spec=pltpu.PrefetchScalarGridSpec(
            num_scalar_prefetch=1,
            grid=(rows // block,),
            in_specs=in_specs,
            out_specs=pl.BlockSpec((block, width), lambda i, c: (first + i, 0)),
        ),
        input_output_aliases=aliases,
        compiler_params=params(),
        cost_estimate=pl.CostEstimate(
            flops=2 * members * tokens * width * rows,
            bytes_accessed=2 * (members + 1) * rows * width,
            transcendentals=0,
        ),
        name="merge",
    )(*args)


def prepare_kernel(members, *refs):
    refs = refs[1:]
    weight, refs = refs[0], refs[1:]
    grads, refs = refs[:members], refs[members:]
    scales, refs = refs[:members], refs[members:]
    tokens, outs = refs[:members], refs[members:]
    numer, factor, others = outs[0], outs[1], outs[2:]
    width = numer.shape[1]
    tile = tile_of(width)
    columns = [scale[:, :1] for scale in scales]
    for at in range(0, width, tile):
        denom = None
        for j in range(members):
            w = jnp.abs(dot(grads[j][...], tokens[j][:, at:at + tile], NN)) * columns[j]
            if j == 0:
                term = w * weight[:, at:at + tile].astype(F32)
                numer[:, at:at + tile] = term.astype(BF16)
            else:
                others[j - 1][:, at:at + tile] = w
            w = w.astype(BF16).astype(F32)
            denom = w if denom is None else denom + w
        factor[:, at:at + tile] = 1.0 / jnp.maximum(denom, 1.0)


def prepare(spot, piece, weight, grads, scales, xs):
    which, start, rows = piece
    members = len(xs)
    tokens = xs[0].shape[0]
    width = weight.shape[1] // members
    block = math.gcd(rows, start, 32)
    first = start // block
    own = pl.BlockSpec((block, width), lambda i, c: (first + i, c[0]))
    in_specs = [own]
    in_specs += [pl.BlockSpec((block, tokens), lambda i, c: (first + i, which))] * members
    in_specs += [pl.BlockSpec((block, LANES), lambda i, c: (first + i, which))] * members
    in_specs += [pl.BlockSpec((tokens, width), lambda i, c: (0, c[0]))] * members
    return pl.pallas_call(
        functools.partial(prepare_kernel, members),
        out_shape=[jax.ShapeDtypeStruct((rows, width), BF16)]
        + [jax.ShapeDtypeStruct((rows, width), F32)] * members,
        grid_spec=pltpu.PrefetchScalarGridSpec(
            num_scalar_prefetch=1,
            grid=(rows // block,),
            in_specs=in_specs,
            out_specs=[pl.BlockSpec((block, width), lambda i, c: (i, 0))] * (members + 1),
        ),
        compiler_params=params(),
        cost_estimate=pl.CostEstimate(
            flops=2 * members * tokens * width * rows,
            bytes_accessed=8 * (members + 1) * rows * width,
            transcendentals=0,
        ),
        name="prepare",
    )(spot, weight, *grads, *scales, *xs)


def finish_kernel(members, numer, factor, *refs):
    others, refs = refs[:members - 1], refs[members - 1:]
    weights, out = refs[:members - 1], refs[-1]
    total = numer[...].astype(F32)
    for w, weight in zip(others, weights):
        total = total + (w[...] * weight[...].astype(F32)).astype(BF16).astype(F32)
    out[...] = (total * factor[...]).astype(BF16)


def finish(piece, ready, received, so_far):
    _, start, rows = piece
    width = so_far.shape[1]
    block = math.gcd(rows, start, 32)
    first = start // block
    args = [*ready, *received]
    return pl.pallas_call(
        functools.partial(finish_kernel, len(ready) - 1),
        out_shape=jax.ShapeDtypeStruct(so_far.shape, BF16),
        grid=(rows // block,),
        in_specs=[pl.BlockSpec((block, width), lambda i: (i, 0))] * len(args)
        + [pl.BlockSpec(memory_space=pl.ANY)],
        out_specs=pl.BlockSpec((block, width), lambda i: (first + i, 0)),
        input_output_aliases={len(args): 0},
        compiler_params=params(),
        cost_estimate=pl.CostEstimate(
            flops=4 * rows * width, bytes_accessed=14 * rows * width, transcendentals=0
        ),
        name="finish",
    )(*args, so_far)


def pieces(units):
    block = rows_of(units)
    count = units // block
    if count < 4:
        return [], [(0, 0, units)], [(1, 0, units)], [], None
    head = block * (count // 2)
    tail = units - block
    return (
        [(0, 0, block)],
        [(0, block, units - block)],
        [(1, 0, head)],
        [(1, head, tail - head)],
        (1, tail, block),
    )


def on_device(n_ckpt, n_fsdp, tokens, gate_weight, up_weight, down_weight, row_code, col_code):
    weights = (gate_weight[0], up_weight[0])
    down = down_weight[0]
    own = tokens[0]
    units, width = down.shape
    part = width // n_ckpt
    spot = lax.axis_index("ckpt")
    core = (lax.axis_index("fsdp") & 1).astype(jnp.int32).reshape(1)
    at = spot.astype(jnp.int32).reshape(1)
    siblings = [(i, i ^ 1) for i in range(n_fsdp)]
    shifts = range(1, n_ckpt)

    def across(value, shift):
        return lax.ppermute(
            value, "ckpt", [(i, (i + shift) % n_ckpt) for i in range(n_ckpt)]
        )

    def cut(which, start, rows):
        lefts = [lax.rem(spot + s, n_ckpt) * part for s in shifts]
        return [lax.dynamic_slice(weights[which], (start, left), (rows, part)) for left in lefts]

    def cut_late(which, start, rows, spot):
        step = math.gcd(rows, 32)
        lefts = [lax.rem(spot + s, n_ckpt) * part for s in shifts]
        return [
            jnp.concatenate([
                lax.dynamic_slice(weights[which], (low, left), (step, part))
                for low in range(start, start + rows, step)
            ]) for left in lefts
        ]

    def send_all(blocks):
        return [across(block, s) for block, s in zip(blocks, shifts)]

    def both(value):
        other = lax.ppermute(value, "fsdp", siblings)
        return jnp.where(
            core[0] == 0, jnp.concatenate([value, other]), jnp.concatenate([other, value])
        )

    first, second, third, late, last = pieces(units)
    arrived = {piece: send_all(cut(*piece)) for piece in first + second + third}

    def have(some, value):
        value, blocks = lax.optimization_barrier((value, [arrived[p] for p in some]))
        arrived.update(zip(some, blocks))
        return value

    plan = hops(n_fsdp)
    plain = [(even, even) for even, _ in plan]
    x = both(gather(
        own, "fsdp", n_fsdp, plan, lambda step, value: have(first, value) if step == 1 else value
    ))
    xs = [x]
    places = gather_order(n_fsdp, plain)
    for s in shifts:
        value = both(gather(across(own, s), "fsdp", n_fsdp, plain))
        value = value.reshape(n_fsdp, *own.shape)
        xs.append(jnp.concatenate(
            [value[places.index(device)] for device in gather_order(n_fsdp, plan)]
        ))

    *kept, send, keep = forward(
        core, x, weights[0], weights[1], down, row_code[0], col_code[0].T
    )
    send, later = lax.optimization_barrier((send, spot))
    got = lax.ppermute(send, "fsdp", siblings)
    total = scatter_sum(add(keep, got), "fsdp", n_fsdp)
    total = gather(total, "fsdp", n_fsdp, plan)
    other = lax.ppermute(total, "fsdp", siblings)
    grads = backward(core, total, other, down, kept)
    all_grads = [grads] + [across(grads, s) for s in shifts]
    blocks, all_grads[1:] = lax.optimization_barrier(
        ([cut_late(*p, later) for p in late], all_grads[1:])
    )
    arrived.update({p: send_all(b) for p, b in zip(late, blocks)})
    scales = [means(grads, x)]
    if last is not None:
        blocks, scales = lax.optimization_barrier((cut_late(*last, later), scales))
        arrived[last] = send_all(blocks)
    scales += [means(g, v) for g, v in zip(all_grads[1:], xs[1:])]

    out = [None, None]
    for piece in first + second + third + late:
        which = piece[0]
        out[which] = merge(
            at, piece, weights[which], arrived[piece], all_grads, scales, xs, out[which]
        )
    if last is not None:
        which = last[0]
        ready = prepare(at, last, weights[which], all_grads, scales, xs)
        ready, out[which] = lax.optimization_barrier((ready, out[which]))
        out[which] = finish(last, ready, arrived[last], out[which])
    return tuple(out)


def solution(mesh):
    in_specs = (
        P("ckpt", "fsdp", None),
        P("ckpt", "fsdp", None),
        P("ckpt", "fsdp", None),
        P("ckpt", "fsdp", None),
        P("ckpt", None, None),
        P("ckpt", None, "fsdp"),
    )
    out_specs = (P("fsdp", "ckpt"), P("fsdp", "ckpt"))
    return jax.shard_map(
        functools.partial(on_device, mesh.shape["ckpt"], mesh.shape["fsdp"]),
        mesh=mesh, in_specs=in_specs, out_specs=out_specs, check_vma=False,
    )
```

```python
import functools
import math

import jax
import jax.numpy as jnp
from jax import lax
from jax.experimental import pallas as pl
from jax.experimental.pallas import tpu as pltpu
from jax.sharding import PartitionSpec as P

F32 = jnp.float32
BF16 = jnp.bfloat16
LANES = 128
NT = (((1,), (1,)), ((), ()))
NN = (((1,), (0,)), ((), ()))
TN = (((0,), (0,)), ((), ()))


def dot(left, right, dims):
    return lax.dot_general(left, right, dims, preferred_element_type=F32)


def params():
    return pltpu.CompilerParams(
        dimension_semantics=("arbitrary",), vmem_limit_bytes=48 * 1024 * 1024
    )


def rows_of(units):
    return 128 if units % 128 == 0 else units


def step_of(rows):
    return max((b for b in range(16, 129, 16) if rows % b == 0), default=rows)


def tile_of(width):
    return 512 if width % 512 == 0 else width


def hops(n):
    high = list(range(1, n.bit_length() - 1))
    return list(zip(high, high[1:] + high[:1]))


def swap(value, axis, n, even, odd):
    pairs = [(i, i ^ (1 << (odd if i & 1 else even))) for i in range(n)]
    return lax.ppermute(value, axis, pairs)


def side(axis, even, odd):
    me = lax.axis_index(axis)
    return jnp.where(me & 1 == 1, (me >> odd) & 1, (me >> even) & 1)


def add(left, right):
    return (left.astype(F32) + right.astype(F32)).astype(BF16)


def scatter_sum(value, axis, n):
    for even, odd in hops(n):
        half = value.shape[0] // 2
        mine = side(axis, even, odd)
        keep = lax.dynamic_slice_in_dim(value, mine * half, half, 0)
        send = lax.dynamic_slice_in_dim(value, (1 - mine) * half, half, 0)
        value = add(keep, swap(send, axis, n, even, odd))
    return value


def gather(value, axis, n, plan, after=lambda step, value: value):
    for step, (even, odd) in enumerate(reversed(plan)):
        other = swap(value, axis, n, even, odd)
        first = side(axis, even, odd) == 0
        value = jnp.where(
            first, jnp.concatenate([value, other]), jnp.concatenate([other, value])
        )
        value = after(step, value)
    return value


def gather_order(n, plan):
    order = []
    for core in (0, 1):
        bits = [pair[core] for pair in reversed(plan)]
        for place in range(n // 2):
            order.append(core + sum(((place >> j) & 1) << b for j, b in enumerate(bits)))
    return order


def forward_kernel(factor, steps, core, x, gate, upper, down, row, col, p, q, act, sd,
                   send, keep, hid, whole, sem):
    step = pl.program_id(0)
    tokens, width = x.shape
    units = gate.shape[0]
    copy = pltpu.make_async_copy(down, whole, sem)

    @pl.when(step == 0)
    def _():
        copy.start()

    a = dot(x[...], gate[...], NT) * factor
    b = dot(x[...], upper[...], NT) * factor
    tile = tile_of(width)
    da = jnp.zeros((tokens, units), F32)
    db = jnp.zeros((tokens, units), F32)
    for at in range(0, width, tile):
        part = x[:, at:at + tile]
        signs = []
        for k in (0, 1):
            code = jnp.bitwise_and(col[:, k:k + 1], row[k:k + 1, at:at + tile])
            odd = jnp.bitwise_and(lax.population_count(code), 1)
            signs.append((1 - 2 * odd).astype(F32).astype(BF16))
        da = da + dot(part, signs[0], NT)
        db = db + dot(part, signs[1], NT)
    da = da * factor
    db = db * factor
    sigma = jax.nn.sigmoid(a)
    s = a * sigma
    slope = sigma * (1.0 + a * (1.0 - sigma))
    curve = sigma * (1.0 - sigma) * (2.0 + a * (1.0 - 2.0 * sigma))
    p[...] = b * slope
    q[...] = db * slope + b * curve * da
    act[...] = s
    sd[...] = slope * da
    hidden = s * b
    d_hidden = slope * da * b + s * db
    even = core[0] == 0
    if steps == 1:
        place = slice(None)
    else:
        place = pl.ds(pl.multiple_of(step * units, units), units)
    hid[:tokens, place] = jnp.where(even, d_hidden, hidden).astype(BF16)
    hid[tokens:, place] = jnp.where(even, hidden, d_hidden).astype(BF16)

    @pl.when(step == steps - 1)
    def _():
        copy.wait()
        for at in range(0, width, tile):
            both = dot(hid[...], whole[:, at:at + tile], NN)
            send[:, at:at + tile] = both[:tokens].astype(BF16)
            keep[:, at:at + tile] = both[tokens:].astype(BF16)


def forward(core, x, gate, upper, down, row, col):
    tokens, width = x.shape
    units = gate.shape[0]
    block = rows_of(units)
    steps = units // block
    by_unit = pl.BlockSpec((block, width), lambda i, c: (i, 0))
    by_lane = pl.BlockSpec((tokens, block), lambda i, c: (0, i))
    fixed = pl.BlockSpec((tokens, width), lambda i, c: (0, 0))
    wide = jax.ShapeDtypeStruct((tokens, units), F32)
    out = jax.ShapeDtypeStruct((tokens, width), BF16)
    return pl.pallas_call(
        functools.partial(forward_kernel, width ** (-0.5), steps),
        out_shape=(wide,) * 4 + (out,) * 2,
        grid_spec=pltpu.PrefetchScalarGridSpec(
            num_scalar_prefetch=1,
            grid=(steps,),
            in_specs=[
                fixed,
                by_unit,
                by_unit,
                pl.BlockSpec(memory_space=pl.ANY),
                pl.BlockSpec((2, width), lambda i, c: (0, 0)),
                pl.BlockSpec((block, 2), lambda i, c: (i, 0)),
            ],
            out_specs=[by_lane] * 4 + [fixed] * 2,
            scratch_shapes=[
                pltpu.VMEM((2 * tokens, units), BF16),
                pltpu.VMEM((units, width), BF16),
                pltpu.SemaphoreType.DMA,
            ],
        ),
        compiler_params=params(),
        cost_estimate=pl.CostEstimate(
            flops=12 * tokens * width * units,
            bytes_accessed=6 * units * width,
            transcendentals=tokens * units,
        ),
        name="forward",
    )(core, x, gate, upper, down, row, col)


def backward_kernel(core, mine, other, down, p, q, act, sd, grads):
    tokens = mine.shape[0]
    g_mine = dot(mine[...], down[...], NT)
    g_other = dot(other[...], down[...], NT)
    even = core[0] == 0
    gh = jnp.where(even, g_mine, g_other)
    gdh = jnp.where(even, g_other, g_mine)
    grads[:, :tokens] = (gdh * p[...] + gh * q[...]).T.astype(BF16)
    grads[:, tokens:] = (gdh * act[...] + gh * sd[...]).T.astype(BF16)


def backward(core, mine, other, down, kept):
    tokens, width = mine.shape
    units = down.shape[0]
    block = rows_of(units)
    by_lane = pl.BlockSpec((tokens, block), lambda i, c: (0, i))
    fixed = pl.BlockSpec((tokens, width), lambda i, c: (0, 0))
    return pl.pallas_call(
        backward_kernel,
        out_shape=jax.ShapeDtypeStruct((units, 2 * tokens), BF16),
        grid_spec=pltpu.PrefetchScalarGridSpec(
            num_scalar_prefetch=1,
            grid=(units // block,),
            in_specs=[
                fixed,
                fixed,
                pl.BlockSpec((block, width), lambda i, c: (i, 0)),
            ] + [by_lane] * 4,
            out_specs=pl.BlockSpec((block, 2 * tokens), lambda i, c: (i, 0)),
        ),
        compiler_params=params(),
        cost_estimate=pl.CostEstimate(
            flops=4 * tokens * width * units,
            bytes_accessed=2 * units * width,
            transcendentals=0,
        ),
        name="backward",
    )(core, mine, other, down, *kept)


def means_kernel(grads, x, scale):
    tokens, width = x.shape
    units = grads.shape[0]
    tile = tile_of(width)
    for k in (0, 1):
        grad = grads[:, k * tokens:(k + 1) * tokens]
        total = jnp.zeros((units, LANES), F32)
        for at in range(0, width, tile):
            e = jnp.abs(dot(grad, x[:, at:at + tile], NN))
            for low in range(0, tile, LANES):
                total = total + e[:, low:low + LANES]
        mean = jnp.sum(total, axis=1, keepdims=True) * (1.0 / width)
        scale[:, k * LANES:(k + 1) * LANES] = jnp.broadcast_to(
            1.0 / (mean + 1e-06), (units, LANES)
        )


def means(grads, x):
    tokens, width = x.shape
    units = grads.shape[0]
    block = rows_of(units)
    return pl.pallas_call(
        means_kernel,
        out_shape=jax.ShapeDtypeStruct((units, 2 * LANES), F32),
        grid=(units // block,),
        in_specs=[
            pl.BlockSpec((block, 2 * tokens), lambda i: (i, 0)),
            pl.BlockSpec((tokens, width), lambda i: (0, 0)),
        ],
        out_specs=pl.BlockSpec((block, 2 * LANES), lambda i: (i, 0)),
        compiler_params=params(),
        cost_estimate=pl.CostEstimate(
            flops=4 * tokens * width * units,
            bytes_accessed=2 * tokens * width,
            transcendentals=0,
        ),
        name="means",
    )(grads, x)


def merge_kernel(members, *refs):
    refs = refs[1:]
    weights, refs = refs[:members], refs[members:]
    grads, refs = refs[:members], refs[members:]
    scales, refs = refs[:members], refs[members:]
    tokens = refs[:members]
    out = refs[-1]
    width = out.shape[1]
    tile = tile_of(width)
    columns = [scale[:, :1] for scale in scales]
    for at in range(0, width, tile):
        numer = denom = None
        for j in range(members):
            hz = dot(grads[j][...], tokens[j][:, at:at + tile], NN)
            w = jnp.abs(hz) * columns[j]
            term = w * weights[j][:, at:at + tile].astype(F32)
            numer = term if numer is None else numer + term
            denom = w if denom is None else denom + w
        out[:, at:at + tile] = (numer / jnp.maximum(denom, 1.0)).astype(BF16)


def merge(spot, piece, weight, received, grads, scales, xs, so_far):
    which, start, rows = piece
    members = len(xs)
    units = weight.shape[0]
    tokens = xs[0].shape[0]
    width = received[0].shape[1]
    block = step_of(math.gcd(rows, start))
    first = start // block
    in_specs = [pl.BlockSpec((block, width), lambda i, c: (first + i, c[0]))]
    in_specs += [pl.BlockSpec((block, width), lambda i, c: (i, 0))] * (members - 1)
    in_specs += [pl.BlockSpec((block, tokens), lambda i, c: (first + i, which))] * members
    in_specs += [pl.BlockSpec((block, LANES), lambda i, c: (first + i, which))] * members
    in_specs += [pl.BlockSpec((tokens, width), lambda i, c: (0, c[0]))] * members
    args = [spot, weight, *received, *grads, *scales, *xs]
    aliases = {}
    if so_far is not None:
        aliases = {len(args): 0}
        in_specs.append(pl.BlockSpec(memory_space=pl.ANY))
        args.append(so_far)
    return pl.pallas_call(
        functools.partial(merge_kernel, members),
        out_shape=jax.ShapeDtypeStruct((units, width), BF16),
        grid_spec=pltpu.PrefetchScalarGridSpec(
            num_scalar_prefetch=1,
            grid=(rows // block,),
            in_specs=in_specs,
            out_specs=pl.BlockSpec((block, width), lambda i, c: (first + i, 0)),
        ),
        input_output_aliases=aliases,
        compiler_params=params(),
        cost_estimate=pl.CostEstimate(
            flops=2 * members * tokens * width * rows,
            bytes_accessed=2 * (members + 1) * rows * width,
            transcendentals=0,
        ),
        name="merge",
    )(*args)


def prepare_kernel(members, *refs):
    refs = refs[1:]
    weight, refs = refs[0], refs[1:]
    grads, refs = refs[:members], refs[members:]
    scales, refs = refs[:members], refs[members:]
    tokens, outs = refs[:members], refs[members:]
    share, others = outs[0], outs[1:]
    width = share.shape[1]
    tile = tile_of(width)
    columns = [scale[:, :1] for scale in scales]
    for at in range(0, width, tile):
        ws = [
            jnp.abs(dot(grads[j][...], tokens[j][:, at:at + tile], NN)) * columns[j]
            for j in range(members)
        ]
        factor = 1.0 / jnp.maximum(sum(ws[1:], ws[0]), 1.0)
        own = ws[0] * weight[:, at:at + tile].astype(F32)
        share[:, at:at + tile] = (own * factor).astype(BF16)
        for other, w in zip(others, ws[1:]):
            other[:, at:at + tile] = (w * factor).astype(BF16)


def prepare(spot, piece, weight, grads, scales, xs):
    which, start, rows = piece
    members = len(xs)
    tokens = xs[0].shape[0]
    width = weight.shape[1] // members
    block = math.gcd(rows, start, 32)
    first = start // block
    own = pl.BlockSpec((block, width), lambda i, c: (first + i, c[0]))
    in_specs = [own]
    in_specs += [pl.BlockSpec((block, tokens), lambda i, c: (first + i, which))] * members
    in_specs += [pl.BlockSpec((block, LANES), lambda i, c: (first + i, which))] * members
    in_specs += [pl.BlockSpec((tokens, width), lambda i, c: (0, c[0]))] * members
    return pl.pallas_call(
        functools.partial(prepare_kernel, members),
        out_shape=[jax.ShapeDtypeStruct((rows, width), BF16)] * members,
        grid_spec=pltpu.PrefetchScalarGridSpec(
            num_scalar_prefetch=1,
            grid=(rows // block,),
            in_specs=in_specs,
            out_specs=[pl.BlockSpec((block, width), lambda i, c: (i, 0))] * members,
        ),
        compiler_params=params(),
        cost_estimate=pl.CostEstimate(
            flops=2 * members * tokens * width * rows,
            bytes_accessed=2 * (members + 1) * rows * width,
            transcendentals=0,
        ),
        name="prepare",
    )(spot, weight, *grads, *scales, *xs)


def finish_kernel(members, share, *refs):
    others, refs = refs[:members - 1], refs[members - 1:]
    weights, out = refs[:members - 1], refs[-1]
    total = share[...].astype(F32)
    for w, weight in zip(others, weights):
        total = total + w[...].astype(F32) * weight[...].astype(F32)
    out[...] = total.astype(BF16)


def finish(piece, ready, received, so_far):
    _, start, rows = piece
    width = so_far.shape[1]
    block = math.gcd(rows, start, 32)
    first = start // block
    args = [*ready, *received]
    return pl.pallas_call(
        functools.partial(finish_kernel, len(ready)),
        out_shape=jax.ShapeDtypeStruct(so_far.shape, BF16),
        grid=(rows // block,),
        in_specs=[pl.BlockSpec((block, width), lambda i: (i, 0))] * len(args)
        + [pl.BlockSpec(memory_space=pl.ANY)],
        out_specs=pl.BlockSpec((block, width), lambda i: (first + i, 0)),
        input_output_aliases={len(args): 0},
        compiler_params=params(),
        cost_estimate=pl.CostEstimate(
            flops=2 * rows * width, bytes_accessed=8 * rows * width, transcendentals=0
        ),
        name="finish",
    )(*args, so_far)


def pieces(units):
    block = rows_of(units)
    count = units // block
    if count < 4:
        return [], [(0, 0, units)], [(1, 0, units)], [], None
    head = block * (count // 2 + 1)
    tail = units - block // 2
    count = -(-(tail - head) // block)
    marks = [head + (tail - head) // 32 * i // count * 32 for i in range(count)] + [tail]
    return (
        [(0, 0, block)],
        [(0, block, units - block)],
        [(1, 0, head)],
        [(1, low, high - low) for low, high in zip(marks, marks[1:])],
        (1, tail, units - tail),
    )


def on_device(n_ckpt, n_fsdp, tokens, gate_weight, up_weight, down_weight, row_code, col_code):
    weights = (gate_weight[0], up_weight[0])
    down = down_weight[0]
    own = tokens[0]
    units, width = down.shape
    part = width // n_ckpt
    spot = lax.axis_index("ckpt")
    core = (lax.axis_index("fsdp") & 1).astype(jnp.int32).reshape(1)
    at = spot.astype(jnp.int32).reshape(1)
    siblings = [(i, i ^ 1) for i in range(n_fsdp)]
    shifts = range(1, n_ckpt)

    def across(value, shift):
        return lax.ppermute(
            value, "ckpt", [(i, (i + shift) % n_ckpt) for i in range(n_ckpt)]
        )

    def cut(which, start, rows):
        lefts = [lax.rem(spot + s, n_ckpt) * part for s in shifts]
        return [lax.dynamic_slice(weights[which], (start, left), (rows, part)) for left in lefts]

    def cut_late(which, start, rows, spot):
        step = math.gcd(rows, 16)
        lefts = [lax.rem(spot + s, n_ckpt) * part for s in shifts]
        return [
            jnp.concatenate([
                lax.dynamic_slice(weights[which], (low, left), (step, part))
                for low in range(start, start + rows, step)
            ]) for left in lefts
        ]

    def send_all(blocks):
        return [across(block, s) for block, s in zip(blocks, shifts)]

    def both(value):
        other = lax.ppermute(value, "fsdp", siblings)
        return jnp.where(
            core[0] == 0, jnp.concatenate([value, other]), jnp.concatenate([other, value])
        )

    first, second, third, late, last = pieces(units)
    arrived = {piece: send_all(cut(*piece)) for piece in first + second + third}

    def have(some, value):
        value, blocks = lax.optimization_barrier((value, [arrived[p] for p in some]))
        arrived.update(zip(some, blocks))
        return value

    plan = hops(n_fsdp)
    plain = [(even, even) for even, _ in plan]
    moved = [across(own, s) for s in shifts]
    start, moved = lax.optimization_barrier((own, moved))
    x = both(gather(
        start, "fsdp", n_fsdp, plan, lambda step, value: have(first, value) if step == 1 else value
    ))
    xs = [x]
    places = gather_order(n_fsdp, plain)
    for value in moved:
        value = both(gather(value, "fsdp", n_fsdp, plain))
        value = value.reshape(n_fsdp, *own.shape)
        xs.append(jnp.concatenate(
            [value[places.index(device)] for device in gather_order(n_fsdp, plan)]
        ))

    *kept, send, keep = forward(
        core, x, weights[0], weights[1], down, row_code[0], col_code[0].T
    )
    send, later = lax.optimization_barrier((send, spot))
    got = lax.ppermute(send, "fsdp", siblings)
    total = scatter_sum(add(keep, got), "fsdp", n_fsdp)
    total = gather(total, "fsdp", n_fsdp, plan)
    other = lax.ppermute(total, "fsdp", siblings)
    grads = backward(core, total, other, down, kept)
    all_grads = [grads] + [across(grads, s) for s in shifts]
    scales = [means(grads, x)]
    blocks, scales = lax.optimization_barrier(([cut_late(*p, later) for p in late], scales))
    arrived.update({p: send_all(b) for p, b in zip(late, blocks)})
    if last is not None:
        blocks, all_grads[1:] = lax.optimization_barrier((cut_late(*last, later), all_grads[1:]))
        arrived[last] = send_all(blocks)
    scales += [means(g, v) for g, v in zip(all_grads[1:], xs[1:])]

    out = [None, None]

    def place(piece):
        which = piece[0]
        out[which] = merge(
            at, piece, weights[which], arrived[piece], all_grads, scales, xs, out[which]
        )

    for piece in first + second + third:
        place(piece)
    if last is not None:
        which = last[0]
        ready = prepare(at, last, weights[which], all_grads, scales, xs)
        for piece in late:
            ready, out, arrived[piece] = lax.optimization_barrier((ready, out, arrived[piece]))
            place(piece)
        out[which] = finish(last, ready, arrived[last], out[which])
    return tuple(out)


def solution(mesh):
    in_specs = (
        P("ckpt", "fsdp", None),
        P("ckpt", "fsdp", None),
        P("ckpt", "fsdp", None),
        P("ckpt", "fsdp", None),
        P("ckpt", None, None),
        P("ckpt", None, "fsdp"),
    )
    out_specs = (P("fsdp", "ckpt"), P("fsdp", "ckpt"))
    return jax.shard_map(
        functools.partial(on_device, mesh.shape["ckpt"], mesh.shape["fsdp"]),
        mesh=mesh, in_specs=in_specs, out_specs=out_specs, check_vma=False,
    )
```

```python
import functools
import math

import jax
import jax.numpy as jnp
from jax import lax
from jax.experimental import pallas as pl
from jax.experimental.pallas import tpu as pltpu
from jax.sharding import PartitionSpec as P

F32 = jnp.float32
BF16 = jnp.bfloat16
LANES = 128
NT = (((1,), (1,)), ((), ()))
NN = (((1,), (0,)), ((), ()))
TN = (((0,), (0,)), ((), ()))


def dot(left, right, dims):
    return lax.dot_general(left, right, dims, preferred_element_type=F32)


def params():
    return pltpu.CompilerParams(
        dimension_semantics=("arbitrary",), vmem_limit_bytes=48 * 1024 * 1024
    )


def rows_of(units):
    return 128 if units % 128 == 0 else units


def step_of(rows, most=128):
    return max((b for b in range(16, most + 1, 16) if rows % b == 0), default=rows)


def tile_of(width):
    return 512 if width % 512 == 0 else width


def hops(n):
    high = list(range(1, n.bit_length() - 1))
    return list(zip(high, high[1:] + high[:1]))


def swap(value, axis, n, even, odd):
    pairs = [(i, i ^ (1 << (odd if i & 1 else even))) for i in range(n)]
    return lax.ppermute(value, axis, pairs)


def side(axis, even, odd):
    me = lax.axis_index(axis)
    return jnp.where(me & 1 == 1, (me >> odd) & 1, (me >> even) & 1)


def add(left, right):
    return (left.astype(F32) + right.astype(F32)).astype(BF16)


def scatter_sum(value, axis, n):
    for even, odd in hops(n):
        half = value.shape[0] // 2
        mine = side(axis, even, odd)
        keep = lax.dynamic_slice_in_dim(value, mine * half, half, 0)
        send = lax.dynamic_slice_in_dim(value, (1 - mine) * half, half, 0)
        value = add(keep, swap(send, axis, n, even, odd))
    return value


def gather(value, axis, n, plan, after=lambda step, value: value):
    for step, (even, odd) in enumerate(reversed(plan)):
        other = swap(value, axis, n, even, odd)
        first = side(axis, even, odd) == 0
        value = jnp.where(
            first, jnp.concatenate([value, other]), jnp.concatenate([other, value])
        )
        value = after(step, value)
    return value


def gather_order(n, plan):
    order = []
    for core in (0, 1):
        bits = [pair[core] for pair in reversed(plan)]
        for place in range(n // 2):
            order.append(core + sum(((place >> j) & 1) << b for j, b in enumerate(bits)))
    return order


def forward_kernel(factor, steps, core, x, gate, upper, down, row, col, p, q, act, sd,
                   send, keep, hid, whole, sem):
    step = pl.program_id(0)
    tokens, width = x.shape
    units = gate.shape[0]
    copy = pltpu.make_async_copy(down, whole, sem)

    @pl.when(step == 0)
    def _():
        copy.start()

    ab = dot(jnp.concatenate([gate[...], upper[...]]), x[...], NT) * factor
    tile = tile_of(width)
    dab = jnp.zeros((2 * units, tokens), F32)
    for at in range(0, width, tile):
        signs = []
        for k in (0, 1):
            code = jnp.bitwise_and(col[:, k:k + 1], row[k:k + 1, at:at + tile])
            odd = jnp.bitwise_and(lax.population_count(code), 1)
            signs.append((1 - 2 * odd).astype(F32).astype(BF16))
        dab = dab + dot(jnp.concatenate(signs), x[:, at:at + tile], NT)
    dab = dab * factor
    a, b = ab[:units], ab[units:]
    da, db = dab[:units], dab[units:]
    sigma = jax.nn.sigmoid(a)
    s = a * sigma
    slope = sigma * (1.0 + a * (1.0 - sigma))
    curve = sigma * (1.0 - sigma) * (2.0 + a * (1.0 - 2.0 * sigma))
    p[...] = b * slope
    q[...] = db * slope + b * curve * da
    act[...] = s
    sd[...] = slope * da
    hidden = s * b
    d_hidden = slope * da * b + s * db
    even = core[0] == 0
    place = pl.ds(pl.multiple_of(step * units, 16), units)
    hid[place, :tokens] = jnp.where(even, d_hidden, hidden)
    hid[place, tokens:] = jnp.where(even, hidden, d_hidden)

    @pl.when(step == steps - 1)
    def _():
        left = hid[...].T.astype(BF16)
        copy.wait()
        for at in range(0, width, tile):
            both = dot(left, whole[:, at:at + tile], NN)
            send[:, at:at + tile] = both[:tokens].astype(BF16)
            keep[:, at:at + tile] = both[tokens:].astype(BF16)


def forward(core, x, gate, upper, down, row, col):
    tokens, width = x.shape
    units = gate.shape[0]
    block = step_of(units, 224)
    steps = units // block
    by_unit = pl.BlockSpec((block, width), lambda i, c: (i, 0))
    by_lane = pl.BlockSpec((block, tokens), lambda i, c: (i, 0))
    fixed = pl.BlockSpec((tokens, width), lambda i, c: (0, 0))
    wide = jax.ShapeDtypeStruct((units, tokens), F32)
    out = jax.ShapeDtypeStruct((tokens, width), BF16)
    return pl.pallas_call(
        functools.partial(forward_kernel, width ** (-0.5), steps),
        out_shape=(wide,) * 4 + (out,) * 2,
        grid_spec=pltpu.PrefetchScalarGridSpec(
            num_scalar_prefetch=1,
            grid=(steps,),
            in_specs=[
                fixed,
                by_unit,
                by_unit,
                pl.BlockSpec(memory_space=pl.ANY),
                pl.BlockSpec((2, width), lambda i, c: (0, 0)),
                pl.BlockSpec((block, 2), lambda i, c: (i, 0)),
            ],
            out_specs=[by_lane] * 4 + [fixed] * 2,
            scratch_shapes=[
                pltpu.VMEM((units, 2 * tokens), F32),
                pltpu.VMEM((units, width), BF16),
                pltpu.SemaphoreType.DMA,
            ],
        ),
        compiler_params=params(),
        cost_estimate=pl.CostEstimate(
            flops=12 * tokens * width * units,
            bytes_accessed=6 * units * width,
            transcendentals=tokens * units,
        ),
        name="forward",
    )(core, x, gate, upper, down, row, col)


def backward_kernel(core, mine, other, down, p, q, act, sd, grads):
    tokens = mine.shape[0]
    g = dot(down[...], jnp.concatenate([mine[...], other[...]]), NT)
    g_mine, g_other = g[:, :tokens], g[:, tokens:]
    even = core[0] == 0
    gh = jnp.where(even, g_mine, g_other)
    gdh = jnp.where(even, g_other, g_mine)
    grads[:, :tokens] = (gdh * p[...] + gh * q[...]).astype(BF16)
    grads[:, tokens:] = (gdh * act[...] + gh * sd[...]).astype(BF16)


def backward(core, mine, other, down, kept):
    tokens, width = mine.shape
    units = down.shape[0]
    block = step_of(units, 448)
    by_lane = pl.BlockSpec((block, tokens), lambda i, c: (i, 0))
    fixed = pl.BlockSpec((tokens, width), lambda i, c: (0, 0))
    return pl.pallas_call(
        backward_kernel,
        out_shape=jax.ShapeDtypeStruct((units, 2 * tokens), BF16),
        grid_spec=pltpu.PrefetchScalarGridSpec(
            num_scalar_prefetch=1,
            grid=(units // block,),
            in_specs=[
                fixed,
                fixed,
                pl.BlockSpec((block, width), lambda i, c: (i, 0)),
            ] + [by_lane] * 4,
            out_specs=pl.BlockSpec((block, 2 * tokens), lambda i, c: (i, 0)),
        ),
        compiler_params=params(),
        cost_estimate=pl.CostEstimate(
            flops=4 * tokens * width * units,
            bytes_accessed=2 * units * width,
            transcendentals=0,
        ),
        name="backward",
    )(core, mine, other, down, *kept)


def means_kernel(grads, x, scale):
    tokens, width = x.shape
    units = grads.shape[0]
    tile = tile_of(width)
    for k in (0, 1):
        grad = grads[:, k * tokens:(k + 1) * tokens]
        total = jnp.zeros((units, LANES), F32)
        for at in range(0, width, tile):
            e = jnp.abs(dot(grad, x[:, at:at + tile], NN))
            for low in range(0, tile, LANES):
                total = total + e[:, low:low + LANES]
        mean = jnp.sum(total, axis=1, keepdims=True) * (1.0 / width)
        scale[:, k * LANES:(k + 1) * LANES] = jnp.broadcast_to(
            1.0 / (mean + 1e-06), (units, LANES)
        )


def means(grads, x):
    tokens, width = x.shape
    units = grads.shape[0]
    block = step_of(units, 448)
    return pl.pallas_call(
        means_kernel,
        out_shape=jax.ShapeDtypeStruct((units, 2 * LANES), F32),
        grid=(units // block,),
        in_specs=[
            pl.BlockSpec((block, 2 * tokens), lambda i: (i, 0)),
            pl.BlockSpec((tokens, width), lambda i: (0, 0)),
        ],
        out_specs=pl.BlockSpec((block, 2 * LANES), lambda i: (i, 0)),
        compiler_params=params(),
        cost_estimate=pl.CostEstimate(
            flops=4 * tokens * width * units,
            bytes_accessed=2 * tokens * width,
            transcendentals=0,
        ),
        name="means",
    )(grads, x)


def merge_kernel(members, *refs):
    refs = refs[1:]
    weights, refs = refs[:members], refs[members:]
    grads, refs = refs[:members], refs[members:]
    scales, refs = refs[:members], refs[members:]
    tokens = refs[:members]
    out = refs[-1]
    width = out.shape[1]
    tile = tile_of(width)
    columns = [scale[:, :1] for scale in scales]
    for at in range(0, width, tile):
        numer = denom = None
        for j in range(members):
            hz = dot(grads[j][...], tokens[j][:, at:at + tile], NN)
            w = jnp.abs(hz) * columns[j]
            term = w * weights[j][:, at:at + tile].astype(F32)
            numer = term if numer is None else numer + term
            denom = w if denom is None else denom + w
        out[:, at:at + tile] = (numer / jnp.maximum(denom, 1.0)).astype(BF16)


def merge(spot, piece, weight, received, grads, scales, xs, so_far):
    which, start, rows = piece
    members = len(xs)
    units = weight.shape[0]
    tokens = xs[0].shape[0]
    width = received[0].shape[1]
    block = step_of(math.gcd(rows, start))
    first = start // block
    in_specs = [pl.BlockSpec((block, width), lambda i, c: (first + i, c[0]))]
    in_specs += [pl.BlockSpec((block, width), lambda i, c: (i, 0))] * (members - 1)
    in_specs += [pl.BlockSpec((block, tokens), lambda i, c: (first + i, which))] * members
    in_specs += [pl.BlockSpec((block, LANES), lambda i, c: (first + i, which))] * members
    in_specs += [pl.BlockSpec((tokens, width), lambda i, c: (0, c[0]))] * members
    args = [spot, weight, *received, *grads, *scales, *xs]
    aliases = {}
    if so_far is not None:
        aliases = {len(args): 0}
        in_specs.append(pl.BlockSpec(memory_space=pl.ANY))
        args.append(so_far)
    return pl.pallas_call(
        functools.partial(merge_kernel, members),
        out_shape=jax.ShapeDtypeStruct((units, width), BF16),
        grid_spec=pltpu.PrefetchScalarGridSpec(
            num_scalar_prefetch=1,
            grid=(rows // block,),
            in_specs=in_specs,
            out_specs=pl.BlockSpec((block, width), lambda i, c: (first + i, 0)),
        ),
        input_output_aliases=aliases,
        compiler_params=params(),
        cost_estimate=pl.CostEstimate(
            flops=2 * members * tokens * width * rows,
            bytes_accessed=2 * (members + 1) * rows * width,
            transcendentals=0,
        ),
        name="merge",
    )(*args)


def prepare_kernel(members, *refs):
    refs = refs[1:]
    weight, refs = refs[0], refs[1:]
    grads, refs = refs[:members], refs[members:]
    scales, refs = refs[:members], refs[members:]
    tokens, outs = refs[:members], refs[members:]
    share, others = outs[0], outs[1:]
    width = share.shape[1]
    tile = tile_of(width)
    columns = [scale[:, :1] for scale in scales]
    for at in range(0, width, tile):
        ws = [
            jnp.abs(dot(grads[j][...], tokens[j][:, at:at + tile], NN)) * columns[j]
            for j in range(members)
        ]
        factor = 1.0 / jnp.maximum(sum(ws[1:], ws[0]), 1.0)
        own = ws[0] * weight[:, at:at + tile].astype(F32)
        share[:, at:at + tile] = (own * factor).astype(BF16)
        for other, w in zip(others, ws[1:]):
            other[:, at:at + tile] = (w * factor).astype(BF16)


def prepare(spot, piece, weight, grads, scales, xs):
    which, start, rows = piece
    members = len(xs)
    tokens = xs[0].shape[0]
    width = weight.shape[1] // members
    block = math.gcd(rows, start, 32)
    first = start // block
    own = pl.BlockSpec((block, width), lambda i, c: (first + i, c[0]))
    in_specs = [own]
    in_specs += [pl.BlockSpec((block, tokens), lambda i, c: (first + i, which))] * members
    in_specs += [pl.BlockSpec((block, LANES), lambda i, c: (first + i, which))] * members
    in_specs += [pl.BlockSpec((tokens, width), lambda i, c: (0, c[0]))] * members
    return pl.pallas_call(
        functools.partial(prepare_kernel, members),
        out_shape=[jax.ShapeDtypeStruct((rows, width), BF16)] * members,
        grid_spec=pltpu.PrefetchScalarGridSpec(
            num_scalar_prefetch=1,
            grid=(rows // block,),
            in_specs=in_specs,
            out_specs=[pl.BlockSpec((block, width), lambda i, c: (i, 0))] * members,
        ),
        compiler_params=params(),
        cost_estimate=pl.CostEstimate(
            flops=2 * members * tokens * width * rows,
            bytes_accessed=2 * (members + 1) * rows * width,
            transcendentals=0,
        ),
        name="prepare",
    )(spot, weight, *grads, *scales, *xs)


def finish_kernel(members, share, *refs):
    others, refs = refs[:members - 1], refs[members - 1:]
    weights, out = refs[:members - 1], refs[-1]
    total = share[...].astype(F32)
    for w, weight in zip(others, weights):
        total = total + w[...].astype(F32) * weight[...].astype(F32)
    out[...] = total.astype(BF16)


def finish(piece, ready, received, so_far):
    _, start, rows = piece
    width = so_far.shape[1]
    block = math.gcd(rows, start, 32)
    first = start // block
    args = [*ready, *received]
    return pl.pallas_call(
        functools.partial(finish_kernel, len(ready)),
        out_shape=jax.ShapeDtypeStruct(so_far.shape, BF16),
        grid=(rows // block,),
        in_specs=[pl.BlockSpec((block, width), lambda i: (i, 0))] * len(args)
        + [pl.BlockSpec(memory_space=pl.ANY)],
        out_specs=pl.BlockSpec((block, width), lambda i: (first + i, 0)),
        input_output_aliases={len(args): 0},
        compiler_params=params(),
        cost_estimate=pl.CostEstimate(
            flops=2 * rows * width, bytes_accessed=8 * rows * width, transcendentals=0
        ),
        name="finish",
    )(*args, so_far)


def pieces(units):
    block = rows_of(units)
    count = units // block
    if count < 4:
        return [], [(0, 0, units)], [(1, 0, units)], [], None
    head = block * (count // 2 + 1) - block // 4
    tail = units - block // 2
    count = -(-(tail - head) // block)
    marks = [head + (tail - head) // 32 * i // count * 32 for i in range(count)] + [tail]
    return (
        [(0, 0, block)],
        [(0, block, units - block)],
        [(1, 0, head)],
        [(1, low, high - low) for low, high in zip(marks, marks[1:])],
        (1, tail, units - tail),
    )


def on_device(n_ckpt, n_fsdp, tokens, gate_weight, up_weight, down_weight, row_code, col_code):
    weights = (gate_weight[0], up_weight[0])
    down = down_weight[0]
    own = tokens[0]
    units, width = down.shape
    part = width // n_ckpt
    spot = lax.axis_index("ckpt")
    core = (lax.axis_index("fsdp") & 1).astype(jnp.int32).reshape(1)
    at = spot.astype(jnp.int32).reshape(1)
    siblings = [(i, i ^ 1) for i in range(n_fsdp)]
    shifts = range(1, n_ckpt)

    def across(value, shift):
        return lax.ppermute(
            value, "ckpt", [(i, (i + shift) % n_ckpt) for i in range(n_ckpt)]
        )

    def cut(which, start, rows):
        lefts = [lax.rem(spot + s, n_ckpt) * part for s in shifts]
        return [lax.dynamic_slice(weights[which], (start, left), (rows, part)) for left in lefts]

    def cut_late(which, start, rows, spot):
        step = math.gcd(rows, 16)
        lefts = [lax.rem(spot + s, n_ckpt) * part for s in shifts]
        return [
            jnp.concatenate([
                lax.dynamic_slice(weights[which], (low, left), (step, part))
                for low in range(start, start + rows, step)
            ]) for left in lefts
        ]

    def send_all(blocks):
        return [across(block, s) for block, s in zip(blocks, shifts)]

    def both(value):
        other = lax.ppermute(value, "fsdp", siblings)
        return jnp.where(
            core[0] == 0, jnp.concatenate([value, other]), jnp.concatenate([other, value])
        )

    first, second, third, late, last = pieces(units)
    arrived = {piece: send_all(cut(*piece)) for piece in first + second + third}

    def have(some, value):
        value, blocks = lax.optimization_barrier((value, [arrived[p] for p in some]))
        arrived.update(zip(some, blocks))
        return value

    plan = hops(n_fsdp)
    plain = [(even, even) for even, _ in plan]
    moved = [across(own, s) for s in shifts]
    start, moved = lax.optimization_barrier((own, moved))
    x = both(gather(
        start, "fsdp", n_fsdp, plan, lambda step, value: have(first, value) if step == 1 else value
    ))
    xs = [x]
    places = gather_order(n_fsdp, plain)
    for value in moved:
        value = both(gather(value, "fsdp", n_fsdp, plain))
        value = value.reshape(n_fsdp, *own.shape)
        xs.append(jnp.concatenate(
            [value[places.index(device)] for device in gather_order(n_fsdp, plan)]
        ))

    *kept, send, keep = forward(
        core, x, weights[0], weights[1], down, row_code[0], col_code[0].T
    )
    send, later = lax.optimization_barrier((send, spot))
    got = lax.ppermute(send, "fsdp", siblings)
    total = scatter_sum(add(keep, got), "fsdp", n_fsdp)
    total = gather(total, "fsdp", n_fsdp, plan)
    other = lax.ppermute(total, "fsdp", siblings)
    grads = backward(core, total, other, down, kept)
    all_grads = [grads] + [across(grads, s) for s in shifts]
    scales = [means(grads, x)]
    blocks, scales = lax.optimization_barrier(([cut_late(*p, later) for p in late], scales))
    arrived.update({p: send_all(b) for p, b in zip(late, blocks)})
    if last is not None:
        blocks, all_grads[1:] = lax.optimization_barrier((cut_late(*last, later), all_grads[1:]))
        arrived[last] = send_all(blocks)
    scales += [means(g, v) for g, v in zip(all_grads[1:], xs[1:])]

    out = [None, None]

    def place(piece):
        which = piece[0]
        out[which] = merge(
            at, piece, weights[which], arrived[piece], all_grads, scales, xs, out[which]
        )

    for piece in first + second + third:
        place(piece)
    if last is not None:
        which = last[0]
        ready = prepare(at, last, weights[which], all_grads, scales, xs)
        for piece in late:
            ready, out, arrived[piece] = lax.optimization_barrier((ready, out, arrived[piece]))
            place(piece)
        out[which] = finish(last, ready, arrived[last], out[which])
    return tuple(out)


def solution(mesh):
    in_specs = (
        P("ckpt", "fsdp", None),
        P("ckpt", "fsdp", None),
        P("ckpt", "fsdp", None),
        P("ckpt", "fsdp", None),
        P("ckpt", None, None),
        P("ckpt", None, "fsdp"),
    )
    out_specs = (P("fsdp", "ckpt"), P("fsdp", "ckpt"))
    return jax.shard_map(
        functools.partial(on_device, mesh.shape["ckpt"], mesh.shape["fsdp"]),
        mesh=mesh, in_specs=in_specs, out_specs=out_specs, check_vma=False,
    )
```

```python
import functools
import math

import jax
import jax.numpy as jnp
from jax import lax
from jax.experimental import pallas as pl
from jax.experimental.pallas import tpu as pltpu
from jax.sharding import PartitionSpec as P

F32 = jnp.float32
BF16 = jnp.bfloat16
LANES = 128
NT = (((1,), (1,)), ((), ()))
NN = (((1,), (0,)), ((), ()))
TN = (((0,), (0,)), ((), ()))


def dot(left, right, dims):
    return lax.dot_general(left, right, dims, preferred_element_type=F32)


def params():
    return pltpu.CompilerParams(
        dimension_semantics=("arbitrary",), vmem_limit_bytes=48 * 1024 * 1024
    )


def rows_of(units):
    return 128 if units % 128 == 0 else units


def step_of(rows, most=128):
    return max((b for b in range(16, most + 1, 16) if rows % b == 0), default=rows)


def tile_of(width):
    return 512 if width % 512 == 0 else width


def hops(n):
    high = list(range(1, n.bit_length() - 1))
    return list(zip(high, high[1:] + high[:1]))


def swap(value, axis, n, even, odd):
    pairs = [(i, i ^ (1 << (odd if i & 1 else even))) for i in range(n)]
    return lax.ppermute(value, axis, pairs)


def side(axis, even, odd):
    me = lax.axis_index(axis)
    return jnp.where(me & 1 == 1, (me >> odd) & 1, (me >> even) & 1)


def add(left, right):
    return (left.astype(F32) + right.astype(F32)).astype(BF16)


def scatter_sum(value, axis, n):
    for even, odd in hops(n):
        half = value.shape[0] // 2
        mine = side(axis, even, odd)
        keep = lax.dynamic_slice_in_dim(value, mine * half, half, 0)
        send = lax.dynamic_slice_in_dim(value, (1 - mine) * half, half, 0)
        value = add(keep, swap(send, axis, n, even, odd))
    return value


def gather(value, axis, n, plan, after=lambda step, value: value):
    for step, (even, odd) in enumerate(reversed(plan)):
        other = swap(value, axis, n, even, odd)
        first = side(axis, even, odd) == 0
        value = jnp.where(
            first, jnp.concatenate([value, other]), jnp.concatenate([other, value])
        )
        value = after(step, value)
    return value


def gather_order(n, plan):
    order = []
    for core in (0, 1):
        bits = [pair[core] for pair in reversed(plan)]
        for place in range(n // 2):
            order.append(core + sum(((place >> j) & 1) << b for j, b in enumerate(bits)))
    return order


def forward_kernel(factor, steps, core, x, gate, upper, down, row, col, p, q, act, sd,
                   send, keep, hid, whole, sem):
    step = pl.program_id(0)
    tokens, width = x.shape
    units = gate.shape[0]
    copy = pltpu.make_async_copy(down, whole, sem)

    @pl.when(step == 0)
    def _():
        copy.start()

    ab = dot(jnp.concatenate([gate[...], upper[...]]), x[...], NT) * factor
    tile = tile_of(width)
    dab = jnp.zeros((2 * units, tokens), F32)
    for at in range(0, width, tile):
        signs = []
        for k in (0, 1):
            code = jnp.bitwise_and(col[:, k:k + 1], row[k:k + 1, at:at + tile])
            odd = jnp.bitwise_and(lax.population_count(code), 1)
            signs.append((1 - 2 * odd).astype(F32).astype(BF16))
        dab = dab + dot(jnp.concatenate(signs), x[:, at:at + tile], NT)
    dab = dab * factor
    a, b = ab[:units], ab[units:]
    da, db = dab[:units], dab[units:]
    sigma = jax.nn.sigmoid(a)
    s = a * sigma
    slope = sigma * (1.0 + a * (1.0 - sigma))
    curve = sigma * (1.0 - sigma) * (2.0 + a * (1.0 - 2.0 * sigma))
    p[...] = b * slope
    q[...] = db * slope + b * curve * da
    act[...] = s
    sd[...] = slope * da
    hidden = s * b
    d_hidden = slope * da * b + s * db
    even = core[0] == 0
    place = pl.ds(pl.multiple_of(step * units, 16), units)
    hid[place, :tokens] = jnp.where(even, d_hidden, hidden)
    hid[place, tokens:] = jnp.where(even, hidden, d_hidden)

    @pl.when(step == steps - 1)
    def _():
        left = hid[...].T.astype(BF16)
        copy.wait()
        for at in range(0, width, tile):
            both = dot(left, whole[:, at:at + tile], NN)
            send[:, at:at + tile] = both[:tokens].astype(BF16)
            keep[:, at:at + tile] = both[tokens:].astype(BF16)


def forward(core, x, gate, upper, down, row, col):
    tokens, width = x.shape
    units = gate.shape[0]
    block = step_of(units, 224)
    steps = units // block
    by_unit = pl.BlockSpec((block, width), lambda i, c: (i, 0))
    by_lane = pl.BlockSpec((block, tokens), lambda i, c: (i, 0))
    fixed = pl.BlockSpec((tokens, width), lambda i, c: (0, 0))
    wide = jax.ShapeDtypeStruct((units, tokens), F32)
    out = jax.ShapeDtypeStruct((tokens, width), BF16)
    return pl.pallas_call(
        functools.partial(forward_kernel, width ** (-0.5), steps),
        out_shape=(wide,) * 4 + (out,) * 2,
        grid_spec=pltpu.PrefetchScalarGridSpec(
            num_scalar_prefetch=1,
            grid=(steps,),
            in_specs=[
                fixed,
                by_unit,
                by_unit,
                pl.BlockSpec(memory_space=pl.ANY),
                pl.BlockSpec((2, width), lambda i, c: (0, 0)),
                pl.BlockSpec((block, 2), lambda i, c: (i, 0)),
            ],
            out_specs=[by_lane] * 4 + [fixed] * 2,
            scratch_shapes=[
                pltpu.VMEM((units, 2 * tokens), F32),
                pltpu.VMEM((units, width), BF16),
                pltpu.SemaphoreType.DMA,
            ],
        ),
        compiler_params=params(),
        cost_estimate=pl.CostEstimate(
            flops=12 * tokens * width * units,
            bytes_accessed=6 * units * width,
            transcendentals=tokens * units,
        ),
        name="forward",
    )(core, x, gate, upper, down, row, col)


def backward_kernel(core, mine, other, down, p, q, act, sd, grads):
    tokens = mine.shape[0]
    g = dot(down[...], jnp.concatenate([mine[...], other[...]]), NT)
    g_mine, g_other = g[:, :tokens], g[:, tokens:]
    even = core[0] == 0
    gh = jnp.where(even, g_mine, g_other)
    gdh = jnp.where(even, g_other, g_mine)
    grads[:, :tokens] = (gdh * p[...] + gh * q[...]).astype(BF16)
    grads[:, tokens:] = (gdh * act[...] + gh * sd[...]).astype(BF16)


def backward(core, mine, other, down, kept):
    tokens, width = mine.shape
    units = down.shape[0]
    block = step_of(units, 448)
    by_lane = pl.BlockSpec((block, tokens), lambda i, c: (i, 0))
    fixed = pl.BlockSpec((tokens, width), lambda i, c: (0, 0))
    return pl.pallas_call(
        backward_kernel,
        out_shape=jax.ShapeDtypeStruct((units, 2 * tokens), BF16),
        grid_spec=pltpu.PrefetchScalarGridSpec(
            num_scalar_prefetch=1,
            grid=(units // block,),
            in_specs=[
                fixed,
                fixed,
                pl.BlockSpec((block, width), lambda i, c: (i, 0)),
            ] + [by_lane] * 4,
            out_specs=pl.BlockSpec((block, 2 * tokens), lambda i, c: (i, 0)),
        ),
        compiler_params=params(),
        cost_estimate=pl.CostEstimate(
            flops=4 * tokens * width * units,
            bytes_accessed=2 * units * width,
            transcendentals=0,
        ),
        name="backward",
    )(core, mine, other, down, *kept)


def means_kernel(grads, x, scale):
    tokens, width = x.shape
    units = grads.shape[0]
    tile = tile_of(width)
    for k in (0, 1):
        grad = grads[:, k * tokens:(k + 1) * tokens]
        total = jnp.zeros((units, LANES), F32)
        for at in range(0, width, tile):
            e = jnp.abs(dot(grad, x[:, at:at + tile], NN))
            for low in range(0, tile, LANES):
                total = total + e[:, low:low + LANES]
        mean = jnp.sum(total, axis=1, keepdims=True) * (1.0 / width)
        scale[:, k * LANES:(k + 1) * LANES] = jnp.broadcast_to(
            1.0 / (mean + 1e-06), (units, LANES)
        )


def means(grads, x):
    tokens, width = x.shape
    units = grads.shape[0]
    block = step_of(units, 448)
    return pl.pallas_call(
        means_kernel,
        out_shape=jax.ShapeDtypeStruct((units, 2 * LANES), F32),
        grid=(units // block,),
        in_specs=[
            pl.BlockSpec((block, 2 * tokens), lambda i: (i, 0)),
            pl.BlockSpec((tokens, width), lambda i: (0, 0)),
        ],
        out_specs=pl.BlockSpec((block, 2 * LANES), lambda i: (i, 0)),
        compiler_params=params(),
        cost_estimate=pl.CostEstimate(
            flops=4 * tokens * width * units,
            bytes_accessed=2 * tokens * width,
            transcendentals=0,
        ),
        name="means",
    )(grads, x)


def merge_kernel(members, *refs):
    refs = refs[1:]
    weights, refs = refs[:members], refs[members:]
    grads, refs = refs[:members], refs[members:]
    scales, refs = refs[:members], refs[members:]
    tokens = refs[:members]
    out = refs[-1]
    width = out.shape[1]
    tile = tile_of(width)
    columns = [scale[:, :1] for scale in scales]
    for at in range(0, width, tile):
        numer = denom = None
        for j in range(members):
            hz = dot(grads[j][...], tokens[j][:, at:at + tile], NN)
            w = jnp.abs(hz) * columns[j]
            term = w * weights[j][:, at:at + tile].astype(F32)
            numer = term if numer is None else numer + term
            denom = w if denom is None else denom + w
        out[:, at:at + tile] = (numer / jnp.maximum(denom, 1.0)).astype(BF16)


def merge(spot, piece, weight, received, grads, scales, xs, so_far):
    which, start, rows = piece
    members = len(xs)
    units = weight.shape[0]
    tokens = xs[0].shape[0]
    width = received[0].shape[1]
    block = step_of(math.gcd(rows, start))
    first = start // block
    in_specs = [pl.BlockSpec((block, width), lambda i, c: (first + i, c[0]))]
    in_specs += [pl.BlockSpec((block, width), lambda i, c: (i, 0))] * (members - 1)
    in_specs += [pl.BlockSpec((block, tokens), lambda i, c: (first + i, which))] * members
    in_specs += [pl.BlockSpec((block, LANES), lambda i, c: (first + i, which))] * members
    in_specs += [pl.BlockSpec((tokens, width), lambda i, c: (0, c[0]))] * members
    args = [spot, weight, *received, *grads, *scales, *xs]
    aliases = {}
    if so_far is not None:
        aliases = {len(args): 0}
        in_specs.append(pl.BlockSpec(memory_space=pl.ANY))
        args.append(so_far)
    return pl.pallas_call(
        functools.partial(merge_kernel, members),
        out_shape=jax.ShapeDtypeStruct((units, width), BF16),
        grid_spec=pltpu.PrefetchScalarGridSpec(
            num_scalar_prefetch=1,
            grid=(rows // block,),
            in_specs=in_specs,
            out_specs=pl.BlockSpec((block, width), lambda i, c: (first + i, 0)),
        ),
        input_output_aliases=aliases,
        compiler_params=params(),
        cost_estimate=pl.CostEstimate(
            flops=2 * members * tokens * width * rows,
            bytes_accessed=2 * (members + 1) * rows * width,
            transcendentals=0,
        ),
        name="merge",
    )(*args)


def prepare_kernel(members, *refs):
    refs = refs[1:]
    weight, refs = refs[0], refs[1:]
    grads, refs = refs[:members], refs[members:]
    scales, refs = refs[:members], refs[members:]
    tokens, outs = refs[:members], refs[members:]
    share, others = outs[0], outs[1:]
    width = share.shape[1]
    tile = tile_of(width)
    columns = [scale[:, :1] for scale in scales]
    for at in range(0, width, tile):
        ws = [
            jnp.abs(dot(grads[j][...], tokens[j][:, at:at + tile], NN)) * columns[j]
            for j in range(members)
        ]
        factor = 1.0 / jnp.maximum(sum(ws[1:], ws[0]), 1.0)
        own = ws[0] * weight[:, at:at + tile].astype(F32)
        share[:, at:at + tile] = (own * factor).astype(BF16)
        for other, w in zip(others, ws[1:]):
            other[:, at:at + tile] = (w * factor).astype(BF16)


def prepare(spot, piece, weight, grads, scales, xs):
    which, start, rows = piece
    members = len(xs)
    tokens = xs[0].shape[0]
    width = weight.shape[1] // members
    block = math.gcd(rows, start, 32)
    first = start // block
    own = pl.BlockSpec((block, width), lambda i, c: (first + i, c[0]))
    in_specs = [own]
    in_specs += [pl.BlockSpec((block, tokens), lambda i, c: (first + i, which))] * members
    in_specs += [pl.BlockSpec((block, LANES), lambda i, c: (first + i, which))] * members
    in_specs += [pl.BlockSpec((tokens, width), lambda i, c: (0, c[0]))] * members
    return pl.pallas_call(
        functools.partial(prepare_kernel, members),
        out_shape=[jax.ShapeDtypeStruct((rows, width), BF16)] * members,
        grid_spec=pltpu.PrefetchScalarGridSpec(
            num_scalar_prefetch=1,
            grid=(rows // block,),
            in_specs=in_specs,
            out_specs=[pl.BlockSpec((block, width), lambda i, c: (i, 0))] * members,
        ),
        compiler_params=params(),
        cost_estimate=pl.CostEstimate(
            flops=2 * members * tokens * width * rows,
            bytes_accessed=2 * (members + 1) * rows * width,
            transcendentals=0,
        ),
        name="prepare",
    )(spot, weight, *grads, *scales, *xs)


def finish_kernel(members, start, parts, share, *refs):
    others, refs = refs[:members - 1], refs[members - 1:]
    weights, refs = refs[:members - 1], refs[members - 1:]
    _, out, made, sems = refs
    rows = share.shape[0] // parts
    copies = []
    for part in range(parts):
        here = pl.ds(part * rows, rows)
        total = share[here, :].astype(F32)
        for w, weight in zip(others, weights):
            total = total + w[here, :].astype(F32) * weight[here, :].astype(F32)
        made[here, :] = total.astype(BF16)
        copies.append(pltpu.make_async_copy(
            made.at[here, :], out.at[pl.ds(start + part * rows, rows), :], sems.at[part]
        ))
        copies[-1].start()
    for copy in copies:
        copy.wait()


def finish(piece, ready, received, so_far):
    _, start, rows = piece
    width = so_far.shape[1]
    parts = 2 if rows % 32 == 0 else 1
    args = [*ready, *received]
    return pl.pallas_call(
        functools.partial(finish_kernel, len(ready), start, parts),
        out_shape=jax.ShapeDtypeStruct(so_far.shape, BF16),
        in_specs=[pl.BlockSpec(memory_space=pltpu.VMEM)] * len(args)
        + [pl.BlockSpec(memory_space=pl.ANY)],
        out_specs=pl.BlockSpec(memory_space=pl.ANY),
        scratch_shapes=[pltpu.VMEM((rows, width), BF16), pltpu.SemaphoreType.DMA((parts,))],
        input_output_aliases={len(args): 0},
        compiler_params=pltpu.CompilerParams(vmem_limit_bytes=16 * 1024 * 1024),
        cost_estimate=pl.CostEstimate(
            flops=2 * rows * width, bytes_accessed=8 * rows * width, transcendentals=0
        ),
        name="finish",
    )(*args, so_far)


def pieces(units):
    block = rows_of(units)
    count = units // block
    if count < 4:
        return [], [(0, 0, units)], [(1, 0, units)], [], None
    head = block * (count // 2 + 1) - block // 4
    tail = units - block // 2
    count = -(-(tail - head) // block)
    marks = [head + (tail - head) // 32 * i // count * 32 for i in range(count)] + [tail]
    return (
        [(0, 0, block)],
        [(0, block, units - block)],
        [(1, 0, head)],
        [(1, low, high - low) for low, high in zip(marks, marks[1:])],
        (1, tail, units - tail),
    )


def on_device(n_ckpt, n_fsdp, tokens, gate_weight, up_weight, down_weight, row_code, col_code):
    weights = (gate_weight[0], up_weight[0])
    down = down_weight[0]
    own = tokens[0]
    units, width = down.shape
    part = width // n_ckpt
    spot = lax.axis_index("ckpt")
    core = (lax.axis_index("fsdp") & 1).astype(jnp.int32).reshape(1)
    at = spot.astype(jnp.int32).reshape(1)
    siblings = [(i, i ^ 1) for i in range(n_fsdp)]
    shifts = range(1, n_ckpt)

    def across(value, shift):
        return lax.ppermute(
            value, "ckpt", [(i, (i + shift) % n_ckpt) for i in range(n_ckpt)]
        )

    def cut(which, start, rows):
        lefts = [lax.rem(spot + s, n_ckpt) * part for s in shifts]
        return [lax.dynamic_slice(weights[which], (start, left), (rows, part)) for left in lefts]

    def cut_late(which, start, rows, spot):
        step = math.gcd(rows, 16)
        lefts = [lax.rem(spot + s, n_ckpt) * part for s in shifts]
        return [
            jnp.concatenate([
                lax.dynamic_slice(weights[which], (low, left), (step, part))
                for low in range(start, start + rows, step)
            ]) for left in lefts
        ]

    def send_all(blocks):
        return [across(block, s) for block, s in zip(blocks, shifts)]

    def both(value):
        other = lax.ppermute(value, "fsdp", siblings)
        return jnp.where(
            core[0] == 0, jnp.concatenate([value, other]), jnp.concatenate([other, value])
        )

    first, second, third, late, last = pieces(units)
    arrived = {piece: send_all(cut(*piece)) for piece in first + second + third}

    def have(some, value):
        value, blocks = lax.optimization_barrier((value, [arrived[p] for p in some]))
        arrived.update(zip(some, blocks))
        return value

    plan = hops(n_fsdp)
    plain = [(even, even) for even, _ in plan]
    moved = [across(own, s) for s in shifts]
    start, moved = lax.optimization_barrier((own, moved))
    x = both(gather(
        start, "fsdp", n_fsdp, plan, lambda step, value: have(first, value) if step == 1 else value
    ))
    xs = [x]
    places = gather_order(n_fsdp, plain)
    for value in moved:
        value = both(gather(value, "fsdp", n_fsdp, plain))
        value = value.reshape(n_fsdp, *own.shape)
        xs.append(jnp.concatenate(
            [value[places.index(device)] for device in gather_order(n_fsdp, plan)]
        ))

    *kept, send, keep = forward(
        core, x, weights[0], weights[1], down, row_code[0], col_code[0].T
    )
    send, later = lax.optimization_barrier((send, spot))
    got = lax.ppermute(send, "fsdp", siblings)
    total = scatter_sum(add(keep, got), "fsdp", n_fsdp)
    total = gather(total, "fsdp", n_fsdp, plan)
    other = lax.ppermute(total, "fsdp", siblings)
    grads = backward(core, total, other, down, kept)
    all_grads = [grads] + [across(grads, s) for s in shifts]
    scales = [means(grads, x)]
    blocks, scales = lax.optimization_barrier(([cut_late(*p, later) for p in late], scales))
    arrived.update({p: send_all(b) for p, b in zip(late, blocks)})
    if last is not None:
        blocks, all_grads[1:] = lax.optimization_barrier((cut_late(*last, later), all_grads[1:]))
        arrived[last] = send_all(blocks)
    scales += [means(g, v) for g, v in zip(all_grads[1:], xs[1:])]

    out = [None, None]

    def place(piece):
        which = piece[0]
        out[which] = merge(
            at, piece, weights[which], arrived[piece], all_grads, scales, xs, out[which]
        )

    for piece in first + second + third:
        place(piece)
    if last is not None:
        which = last[0]
        ready = prepare(at, last, weights[which], all_grads, scales, xs)
        for piece in late:
            ready, out, arrived[piece] = lax.optimization_barrier((ready, out, arrived[piece]))
            place(piece)
        out[which] = finish(last, ready, arrived[last], out[which])
    return tuple(out)


def solution(mesh):
    in_specs = (
        P("ckpt", "fsdp", None),
        P("ckpt", "fsdp", None),
        P("ckpt", "fsdp", None),
        P("ckpt", "fsdp", None),
        P("ckpt", None, None),
        P("ckpt", None, "fsdp"),
    )
    out_specs = (P("fsdp", "ckpt"), P("fsdp", "ckpt"))
    return jax.shard_map(
        functools.partial(on_device, mesh.shape["ckpt"], mesh.shape["fsdp"]),
        mesh=mesh, in_specs=in_specs, out_specs=out_specs, check_vma=False,
    )
```
